128 devices in a mesh: gx: 4 (over x), gy: 4 (over y), gz: 8 (over z, core).
Axes of the slice: x: 4, y: 4, z: 4, core: 2. Of those that a mesh axis runs over, the one named last changes fastest.
Arguments:
- coarse_velocity: float32 [3, 64, 64, 1024], P(None, 'gx', 'gy', 'gz'), may hold values from -6 to 6
- coarse_viscosity: float32 [64, 64, 1024], P('gx', 'gy', 'gz'), may hold values from 0.1 to 3
- coarse_rhs: float32 [3, 64, 64, 1024], P(None, 'gx', 'gy', 'gz'), may hold values from -6 to 6
- fine_velocity: float32 [128, 4, 3, 32768], P(('gx', 'gy', 'gz')), may hold values from -6 to 6
- fine_rhs: float32 [128, 4, 3, 32768], P(('gx', 'gy', 'gz')), may hold values from -6 to 6
- fine_viscosity: float32 [128, 4, 32768], P(('gx', 'gy', 'gz')), may hold values from 0.1 to 3
- refined: int32 [128, 2], P(('gx', 'gy', 'gz')), may hold values from 0 to 7, as said below
- owner: int32 [128, 2], P(('gx', 'gy', 'gz')), may hold values from 0 to 127, as said below
Outputs:
- fine_out: float32 [128, 4, 3, 32768], P(('gx', 'gy', 'gz'))
- coarse_synced: float32 [3, 64, 64, 1024], P(None, 'gx', 'gy', 'gz')
- coarse_residual: float32 [3, 64, 64, 1024], P(None, 'gx', 'gy', 'gz')
The draws below stay inside these ranges and needn't reach their ends.
Inputs may be any that keep to these rules, and one draw needn't show every extreme that they name: `refined`: each row holds 2 different positions. Row h names 2 different owners of home h's patches, all with the same indices along gy and gz as home h. Among the homes that share their indices along gy and gz, one owner is named in every row, so that all of its 4 slots hold patches.
All inputs are finite; a program needn't handle non-finite values.
Results may differ from the reference program's by a relative error of at most 0.00002.
Values sent between devices are 32-bit elements; how exact they have to be, the bound alone decides.
A program may use at most 192 MiB of HBM per device.

```python
import math
import jax
import jax.numpy as jnp
import numpy as np
from jax import lax

PE = 32
SWEEPS = 2
CAP = 1
HOMED = 2
CX = 16
CY = 16
CZ = 128
HOMES = 128
SLOTS = 4
CELLS = 32768
POSITIONS = 8
NX = 64
NY = 64
NZ = 1024
N_GY = 4
N_GZ = 8


def draw_refined(key, part):
    key = jax.random.fold_in(key, 11)
    row_keys = jax.random.split(key, HOMES)

    def one_row(row_key):
        return jax.random.permutation(row_key, POSITIONS)[:HOMED]
    return jax.vmap(one_row)(row_keys).astype(jnp.int32)


def draw_owner(key, part):
    key = jax.random.fold_in(key, 23)
    group_total = SLOTS // CAP
    plane_total = HOMES // group_total
    hot_groups = jax.random.randint(jax.random.fold_in(key, 1), (plane_total,), 0, group_total).astype(jnp.int32)
    row_keys = jax.random.split(jax.random.fold_in(key, 2), HOMES)
    home_numbers = jnp.arange(HOMES, dtype=jnp.int32)

    def one_row(row_key, home_number):
        first_key, second_key = jax.random.split(row_key)
        plane = home_number % plane_total
        hot_group = hot_groups[plane]
        tickets = jax.random.permutation(first_key, group_total - 1)[:HOMED - 1].astype(jnp.int32)
        others = tickets + (tickets >= hot_group).astype(jnp.int32)
        groups = jnp.concatenate([jnp.reshape(hot_group, (1,)), others])
        row_values = groups * plane_total + plane
        return jax.random.permutation(second_key, row_values)
    return jax.vmap(one_row)(row_keys, home_numbers).astype(jnp.int32)


def level_of(stream_key, extent, cuts, least, high):
    loudness, own = 1.0, jax.random.fold_in(stream_key, 6)
    for axis_at, parts in cuts:
        draws = jnp.exp(jax.random.uniform(jax.random.fold_in(own, axis_at), (parts,), jnp.float32, least / len(cuts), high / len(cuts)))
        loudness = loudness * jnp.repeat(draws, extent[axis_at] // parts).reshape([-1 if axis == axis_at else 1 for axis in range(len(extent))])
    return loudness


def bell_draw(stream_key, dims, width, reach, cuts=(), kind=jnp.bfloat16):
    loudness = level_of(stream_key, dims, cuts, -0.22, 0.18) if cuts else 1.0
    entries = jax.random.normal(stream_key, dims, jnp.float32) * width * loudness
    return jnp.minimum(jnp.maximum(entries, -reach), reach).astype(kind)


def setup_inputs(seed: int = 0) -> dict:
    key_list = jax.random.split(jax.random.key(seed), 9)
    return {
        "coarse_velocity": bell_draw(key_list[0], (3, NX, NY, NZ), 1.0, 6.0, ((1, 4), (2, 4), (3, 8)), jnp.float32),
        "coarse_viscosity": jnp.clip(jnp.exp(math.log(3.0) - 3.4011974 * jax.random.uniform(key_list[1], (NX, NY, NZ), jnp.float32) ** level_of(key_list[1], (NX, NY, NZ), ((0, 4), (1, 4), (2, 8)), -0.2, 0.2)), 0.1, 3.0),
        "coarse_rhs": bell_draw(key_list[2], (3, NX, NY, NZ), 1.0, 6.0, ((1, 4), (2, 4), (3, 8)), jnp.float32),
        "fine_velocity": bell_draw(key_list[3], (HOMES, SLOTS, 3, CELLS), 1.0, 6.0, ((0, 128),), jnp.float32),
        "fine_rhs": bell_draw(key_list[4], (HOMES, SLOTS, 3, CELLS), 1.0, 6.0, ((0, 128),), jnp.float32),
        "fine_viscosity": jnp.clip(jnp.exp(math.log(3.0) - 3.4011974 * jax.random.uniform(key_list[5], (HOMES, SLOTS, CELLS), jnp.float32) ** level_of(key_list[5], (HOMES, SLOTS, CELLS), ((0, 128),), -0.2, 0.2)), 0.1, 3.0),
        "refined": draw_refined(jax.random.fold_in(key_list[8], 71), 0),
        "owner": draw_owner(jax.random.fold_in(key_list[8], 71), 0),
    }


reaction = 1.0


def patch_tables(patch_edge):
    cell_count = patch_edge * patch_edge * patch_edge
    numbers = np.arange(cell_count)
    position = (numbers // (patch_edge * patch_edge), (numbers // patch_edge) % patch_edge, numbers % patch_edge)
    offsets = []
    inside = np.zeros((6, cell_count))
    for axis_number in range(3):
        stride = [patch_edge * patch_edge, patch_edge, 1][axis_number]
        for facing in range(2):
            direction = 2 * axis_number + facing
            offsets.append(stride if facing == 1 else -stride)
            at_border = position[axis_number] == (patch_edge - 1 if facing == 1 else 0)
            inside[direction] = np.where(at_border, 0.0, 1.0)
    colour = (position[0] + position[1] + position[2]) % 2 == 0
    return offsets, inside, colour


def rim_offsets(coarse_edge, stride_first, stride_second):
    offsets = []
    for axis_number in range(3):
        others = [index_value for index_value in range(3) if index_value != axis_number]
        for facing in range(2):
            layer_at = -1 if facing == 0 else coarse_edge
            for first_cell in range(coarse_edge):
                for second_cell in range(coarse_edge):
                    location = [0, 0, 0]
                    location[axis_number] = layer_at
                    location[others[0]] = first_cell
                    location[others[1]] = second_cell
                    offsets.append(location[0] * stride_first + location[1] * stride_second + location[2])
    return np.array(offsets)


def cell_offsets(coarse_edge, stride_first, stride_second):
    offsets = []
    for first_cell in range(coarse_edge):
        for second_cell in range(coarse_edge):
            for third_cell in range(coarse_edge):
                offsets.append(first_cell * stride_first + second_cell * stride_second + third_cell)
    return np.array(offsets)


def shifted(values, offset):
    if offset > 0:
        filler = jnp.zeros(values.shape[:-1] + (offset,), values.dtype)
        return jnp.concatenate([values[..., offset:], filler], axis=-1)
    filler = jnp.zeros(values.shape[:-1] + (-offset,), values.dtype)
    return jnp.concatenate([filler, values[..., :offset]], axis=-1)


def neighbours(loaded, weights, offsets, state):
    total = loaded
    for direction in range(6):
        total = total + weights[direction][:, None, :] * shifted(state, offsets[direction])
    return total


def ghost_field(face, axis_number, facing):
    upsampled = jnp.repeat(jnp.repeat(face, 2, axis=1), 2, axis=2)
    upsampled = jnp.moveaxis(upsampled, 3, 1)
    widened = jnp.expand_dims(upsampled, 2 + axis_number)
    padding = [(0, 0), (0, 0), (0, 0), (0, 0), (0, 0)]
    padding[2 + axis_number] = (0, PE - 1) if facing == 0 else (PE - 1, 0)
    return jnp.pad(widened, padding).reshape(face.shape[0], 4, -1)


def smooth_patches(rim_values, velocity, forcing, viscosity):
    offsets, inside, colour = patch_tables(PE)
    slot_count = velocity.shape[0]
    coarse_edge = PE // 2
    faces = rim_values.reshape(slot_count, 6, coarse_edge, coarse_edge, 4)
    diagonal = jnp.full(viscosity.shape, reaction, jnp.float32)
    loaded = forcing
    weights = []
    for direction in range(6):
        ghost = ghost_field(faces[:, direction], direction // 2, direction % 2)
        interior = jnp.asarray(inside[direction], jnp.float32)
        face_weight = 0.5 * (viscosity + interior * shifted(viscosity, offsets[direction]) + ghost[:, 3])
        diagonal = diagonal + face_weight
        loaded = loaded + face_weight[:, None, :] * ghost[:, :3]
        weights.append(face_weight * interior)
    red_cells = jnp.asarray(colour)
    state = velocity
    for sweep_number in range(SWEEPS):
        for parity in (red_cells, jnp.logical_not(red_cells)):
            update = neighbours(loaded, weights, offsets, state) / diagonal[:, None, :]
            state = jnp.where(parity, update, state)
    residual = neighbours(loaded, weights, offsets, state) - diagonal[:, None, :] * state
    joined = jnp.concatenate([residual, state], axis=1)
    blocks = joined.reshape(slot_count, 6, coarse_edge, 2, coarse_edge, 2, coarse_edge, 2)
    averaged = 0.125 * jnp.sum(blocks, axis=(3, 5, 7))
    return state, averaged.reshape(slot_count, -1)


def coarse_residual(padded_velocity, padded_viscosity, rhs_values):
    middle = (slice(1, -1), slice(1, -1), slice(1, -1))
    centre_velocity = padded_velocity[(slice(None),) + middle]
    centre_viscosity = padded_viscosity[middle]
    applied = reaction * centre_velocity
    for axis_number in range(3):
        for step_size in (2, 0):
            window = list(middle)
            window[axis_number] = slice(step_size, step_size + centre_viscosity.shape[axis_number])
            window = tuple(window)
            face_weight = 0.5 * (centre_viscosity + padded_viscosity[window])
            applied = applied + 0.25 * face_weight * (centre_velocity - padded_velocity[(slice(None),) + window])
    return rhs_values - applied


def reference(coarse_velocity, coarse_viscosity, coarse_rhs, fine_velocity, fine_rhs, fine_viscosity, refined, owner):
    coarse_edge = PE // 2
    stacked = jnp.concatenate([coarse_velocity, coarse_viscosity[None]], axis=0)
    padded = jnp.pad(stacked, ((0, 0), (1, 1), (1, 1), (1, 1)))
    second_plane = NY + 2
    third_plane = NZ + 2
    home_rows = jnp.arange(HOMES, dtype=jnp.int32)[:, None]
    first_block = home_rows // (N_GY * N_GZ)
    second_block = (home_rows // N_GZ) % N_GY
    third_block = home_rows % N_GZ
    second_count = CY // coarse_edge
    third_count = CZ // coarse_edge
    first_anchor = first_block * CX + (refined // (second_count * third_count)) * coarse_edge
    second_anchor = second_block * CY + ((refined // third_count) % second_count) * coarse_edge
    third_anchor = third_block * CZ + (refined % third_count) * coarse_edge
    base_index = (first_anchor + 1) * (second_plane * third_plane) + (second_anchor + 1) * third_plane + third_anchor + 1
    rim_table = jnp.asarray(rim_offsets(coarse_edge, second_plane * third_plane, third_plane), jnp.int32)
    rim_index = base_index[:, :, None] + rim_table[None, None, :]
    columns = padded.reshape(4, -1).T
    rim_values = columns[rim_index].reshape(HOMES, HOMED, -1)
    patch_order = jnp.arange(HOMED, dtype=jnp.int32)
    earlier = (owner[:, None, :] == owner[:, :, None]) & (patch_order[None, None, :] < patch_order[None, :, None])
    rank_in_row = jnp.sum(earlier.astype(jnp.int32), axis=2)
    slot_index = (home_rows // (N_GY * N_GZ)) * CAP + rank_in_row
    rim_slots = jnp.zeros((HOMES, SLOTS, rim_values.shape[-1]), jnp.float32).at[owner, slot_index].set(rim_values)
    occupied = jnp.zeros((HOMES, SLOTS), jnp.float32).at[owner, slot_index].set(1.0)

    def one_owner(inputs):
        return smooth_patches(inputs[0], inputs[1], inputs[2], inputs[3])

    smoothed, averaged = lax.map(one_owner, (rim_slots, fine_velocity, fine_rhs, fine_viscosity))
    fine_out = smoothed * occupied[:, :, None, None]
    patch_average = averaged[owner, slot_index].reshape(HOMES, HOMED, 6, coarse_edge * coarse_edge * coarse_edge)
    cell_base = (first_anchor * NY + second_anchor) * NZ + third_anchor
    cell_table = jnp.asarray(cell_offsets(coarse_edge, NY * NZ, NZ), jnp.int32)
    cell_index = (cell_base[:, :, None] + cell_table[None, None, :]).reshape(-1)
    mean_residual = jnp.moveaxis(patch_average[:, :, :3], 2, 0).reshape(3, -1)
    mean_velocity = jnp.moveaxis(patch_average[:, :, 3:], 2, 0).reshape(3, -1)
    synced = coarse_velocity.reshape(3, -1).at[:, cell_index].set(mean_velocity).reshape(coarse_velocity.shape)
    padded_synced = jnp.pad(synced, ((0, 0), (1, 1), (1, 1), (1, 1)))
    residual = coarse_residual(padded_synced, padded[3], coarse_rhs)
    residual = residual.reshape(3, -1).at[:, cell_index].set(mean_residual).reshape(coarse_rhs.shape)
    return fine_out, synced, residual
```

```python
import functools

import jax
import jax.numpy as jnp
from jax import lax
from jax.experimental import pallas as pl
from jax.experimental.pallas import tpu as pltpu
from jax.sharding import PartitionSpec as P

SWEEPS = 2
EDGE = 16
SLOTS = 4
REACTION = 1.0
TILE = (8, 128)
SLAB = (16, 128)
MESH = pl.DeviceIdType.MESH
AXES = ("gx", "gy", "gz")


def lane_take(values, index):
    numbers = lax.GatherDimensionNumbers(
        offset_dims=(),
        collapsed_slice_dims=(1,),
        start_index_map=(1,),
        operand_batching_dims=(0,),
        start_indices_batching_dims=(0,),
    )
    return lax.gather(
        values,
        index[..., None],
        numbers,
        slice_sizes=(1, 1),
        mode=lax.GatherScatterMode.PROMISE_IN_BOUNDS,
    )


def push(source, target, sent, landed, device):
    return pltpu.make_async_remote_copy(
        src_ref=source,
        dst_ref=target,
        send_sem=sent,
        recv_sem=landed,
        device_id=device,
        device_id_type=MESH,
    )


def kernel(
    cv, cm, cr, fv, fr, fm, place, own,
    fo, so, ro,
    C, CR, FV, FR, FM, HX, HY, HZ, EF, ZF, MSG, RIM, PV, U, LD, W, GY, RB,
    MEAN, RET, SP, RM, HX2, HY2, HZ2, ZF2,
    lsem, asend, arecv, bsend, brecv, csend, crecv, dsend, drecv,
):
    at = [lax.axis_index(axis) for axis in AXES]
    size = [lax.axis_size(axis) for axis in AXES]
    me, peers = at[0], size[0]

    def beside(number, step):
        return {AXES[number]: lax.rem(at[number] + (step + size[number]), size[number])}

    loads = [
        pltpu.make_async_copy(cv, C.at[0:3, 1 : EDGE + 1], lsem.at[0]),
        pltpu.make_async_copy(cm, C.at[3, 1 : EDGE + 1], lsem.at[1]),
        pltpu.make_async_copy(fm, FM, lsem.at[2]),
        pltpu.make_async_copy(fr, FR, lsem.at[3]),
        pltpu.make_async_copy(fv, FV, lsem.at[4]),
        pltpu.make_async_copy(cr, CR, lsem.at[5]),
    ]
    for load in loads:
        load.start()

    barrier = pltpu.get_barrier_semaphore()
    for step in range(1, peers):
        pl.semaphore_signal(barrier, inc=1, device_id=beside(0, step), device_id_type=MESH)
    for number in (1, 2):
        for step in (1, -1):
            pl.semaphore_signal(
                barrier, inc=1, device_id=beside(number, step), device_id_type=MESH
            )
    pl.semaphore_wait(barrier, peers + 3)

    lane = lax.broadcasted_iota(jnp.int32, TILE, 1)
    row = lax.broadcasted_iota(jnp.int32, TILE, 0)
    third = lane & 31
    quarter = lane >> 5
    even = ((third + quarter) & 1) == 0
    z_first, z_last = third == 0, third == 31
    y_first = (row == 0) & (quarter == 0)
    y_last = (row == 7) & (quarter == 3)
    lane16 = lax.broadcasted_iota(jnp.int32, SLAB, 1)
    row16 = lax.broadcasted_iota(jnp.int32, SLAB, 0)
    group16 = lane16 >> 4
    inner16 = lane16 & 15
    positions = [place[0, 0], place[0, 1]]
    groups = [lax.div(own[0, i], size[1] * size[2]) for i in range(2)]

    def faces(block, planes, hx, hy, hz, packed, sent, landed):
        first, last = 1, EDGE
        return [
            push(block.at[:, last], hx.at[0], sent.at[0], landed.at[0], beside(0, 1)),
            push(block.at[:, first], hx.at[1], sent.at[1], landed.at[1], beside(0, -1)),
            push(block.at[:, planes, EDGE - 1], hy.at[0], sent.at[2], landed.at[2], beside(1, 1)),
            push(block.at[:, planes, 0], hy.at[1], sent.at[3], landed.at[3], beside(1, -1)),
            push(packed, hz.at[0], sent.at[4], landed.at[4], beside(2, 1)),
            push(packed, hz.at[1], sent.at[5], landed.at[5], beside(2, -1)),
        ]

    loads[0].wait()
    loads[1].wait()
    outward = faces(C, pl.ds(1, EDGE), HX, HY, HZ, ZF, asend, arecv)
    for copy in outward[:4]:
        copy.start()
    packed = jnp.zeros(SLAB, jnp.float32)
    for c in range(4):
        upper = jnp.zeros(SLAB, jnp.float32)
        lower = jnp.zeros(SLAB, jnp.float32)
        for x in range(EDGE):
            plane = C[c, x + 1]
            here = inner16 == x
            upper = jnp.where(here, pltpu.roll(plane, (x - 15) % 128, 1), upper)
            lower = jnp.where(here, pltpu.roll(plane, x, 1), lower)
        EF[0, c] = upper
        EF[1, c] = lower
        turn = (32 * c + 16) % 128
        packed = jnp.where(group16 == 2 * c, pltpu.roll(upper, turn, 1), packed)
        packed = jnp.where(group16 == 2 * c + 1, pltpu.roll(lower, turn, 1), packed)
    ZF[...] = packed
    for copy in outward[4:]:
        copy.start()

    loads[2].wait()
    loads[3].wait()
    loads[4].wait()

    def pack(j, carry):
        def pair(ref, start):
            low = ref[pl.ds(start + 64 * j, 8, stride=SLOTS), :]
            high = ref[pl.ds(start + 64 * j + 32, 8, stride=SLOTS), :]
            return jnp.where(even, low, high), jnp.where(even, high, low)

        for s in range(SLOTS):
            PV[s, 0, j + 1], PV[s, 1, j + 1] = pair(FM, s)
            for c in range(3):
                LD[s, 0, c, j], LD[s, 1, c, j] = pair(FR, c * 1024 + s)
                U[s, 0, c, j + 1], U[s, 1, c, j + 1] = pair(FV, c * 1024 + s)
        return carry

    lax.fori_loop(0, EDGE, pack, 0)

    for copy in outward:
        copy.wait_recv()
    for number, halo in ((0, HX), (1, HY)):
        for facing in range(2):
            outside = at[number] == (size[number] - 1 if facing else 0)
            halo[facing] = jnp.where(outside, 0.0, halo[facing])
    for facing in range(2):
        outside = at[2] == (size[2] - 1 if facing else 0)
        HZ[facing] = jnp.where(outside, 0.0, HZ[facing])

    odd_group = (group16 & 1) == 1
    across = jnp.where(odd_group, HZ[1], HZ[0])
    rims = []
    for i in range(2):
        p = positions[i]
        parts = [jnp.zeros(SLAB, jnp.float32)] * 3
        for c in range(4):
            for facing in range(2):
                g = 2 * c + facing
                here = group16 == g
                turn = (16 * g - 16 * p) & 127
                turn_z = (16 * g - 16 * p + (-16 if facing else 16)) & 127
                parts = [
                    jnp.where(here, pltpu.roll(HX[facing, c], turn, 1), parts[0]),
                    jnp.where(here, pltpu.roll(HY[facing, c], turn, 1), parts[1]),
                    jnp.where(here, pltpu.roll(EF[facing, c], turn_z, 1), parts[2]),
                ]
        parts[2] = jnp.where(jnp.where(odd_group, p - 7, p) == 0, across, parts[2])
        rims.append(parts)
    for peer in range(peers):
        is_first = jnp.full(SLAB, groups[0], jnp.int32) == peer
        for k in range(3):
            MSG[peer, 16 * k : 16 * k + 16] = jnp.where(is_first, rims[0][k], rims[1][k])
        first = jnp.full(TILE, groups[0], jnp.int32) == peer
        second = jnp.full(TILE, groups[1], jnp.int32) == peer
        MSG[peer, 48:56] = jnp.where(first | second, 1.0, 0.0)
    out_rims = []
    for step in range(1, peers):
        peer = lax.rem(me + step, peers)
        out_rims.append(
            push(
                MSG.at[peer], RIM.at[me], bsend.at[step - 1], brecv.at[step - 1], beside(0, step)
            )
        )
        out_rims[-1].start()
    RIM[me] = MSG[me]

    def y_up(tile):
        turned = pltpu.roll(tile, 96, 1)
        return jnp.where(quarter == 3, pltpu.roll(turned, 7, 0), turned)

    def y_down(tile):
        turned = pltpu.roll(tile, 32, 1)
        return jnp.where(quarter == 0, pltpu.roll(turned, 1, 0), turned)

    def far(colour, before, after):
        if colour == 0:
            return jnp.where(even, before, after)
        return jnp.where(even, after, before)

    def total(s, colour, c, j, weights):
        other = U.at[s, 1 - colour, c]
        tile = other[j + 1]
        return (
            LD[s, colour, c, j]
            + weights[0] * tile
            + weights[1] * far(colour, other[j], other[j + 2])
            + weights[2] * y_down(tile)
            + weights[3] * y_up(tile)
            + weights[4] * pltpu.roll(tile, 1, 1)
            + weights[5] * pltpu.roll(tile, 127, 1)
        )

    def one_slot(turn, carry):
        s = lax.rem(me + (2 * peers - turn), peers)

        @pl.when(turn < peers)
        def _():
            push(
                MSG.at[s], RIM.at[s], bsend.at[turn - 1], brecv.at[turn - 1], beside(0, 1)
            ).wait_recv()

        high_half = quarter >= 2
        x_rows = [RIM[s, pl.ds(h, 8, stride=2), :] for h in range(2)]
        z_rows = [RIM[s, pl.ds(32 + h, 8, stride=2), :] for h in range(2)]
        y_slab = RIM[s, 16:32]
        for c in range(4):
            for facing in range(2):
                index = 16 * (2 * c + facing) + (third >> 1)
                ghost = jnp.where(
                    high_half, lane_take(x_rows[1], index), lane_take(x_rows[0], index)
                )
                for colour in range(2):
                    if c == 3:
                        PV[s, colour, facing * 17] = ghost
                    else:
                        U[s, colour, c, facing * 17] = ghost
            index = 32 * c + jnp.where((lane16 >> 5) == 3, 16, 0) + ((lane16 & 31) >> 1)
            GY[c] = lane_take(y_slab, index)

        def prepare(j, carry):
            ghost_z, ghost_y = [], []
            for c in range(4):
                index = 32 * c + j + jnp.where(z_last, 16, 0)
                ghost_z.append(
                    jnp.where(high_half, lane_take(z_rows[1], index), lane_take(z_rows[0], index))
                )
                ghost_y.append(jnp.broadcast_to(GY[c, pl.ds(j, 1), :], TILE))
            for colour in range(2):
                own_tile = PV[s, colour, j + 1]
                other = PV.at[s, 1 - colour]
                tile = other[j + 1]
                beside_it = [
                    tile,
                    far(colour, other[j], other[j + 2]),
                    jnp.where(y_first, ghost_y[3], y_down(tile)),
                    jnp.where(y_last, ghost_y[3], y_up(tile)),
                    jnp.where(z_first, ghost_z[3], pltpu.roll(tile, 1, 1)),
                    jnp.where(z_last, ghost_z[3], pltpu.roll(tile, 127, 1)),
                ]
                face = [0.5 * (own_tile + value) for value in beside_it]
                diagonal = REACTION + face[0]
                for value in face[1:]:
                    diagonal = diagonal + value
                rim_y = jnp.where(y_first, face[2], jnp.where(y_last, face[3], 0.0))
                rim_z = jnp.where(z_first, face[4], jnp.where(z_last, face[5], 0.0))
                for c in range(3):
                    LD[s, colour, c, j] = (
                        LD[s, colour, c, j] + rim_y * ghost_y[c] + rim_z * ghost_z[c]
                    )
                W[colour, j, 0] = face[0]
                W[colour, j, 1] = face[1]
                W[colour, j, 2] = jnp.where(y_first, 0.0, face[2])
                W[colour, j, 3] = jnp.where(y_last, 0.0, face[3])
                W[colour, j, 4] = jnp.where(z_first, 0.0, face[4])
                W[colour, j, 5] = jnp.where(z_last, 0.0, face[5])
                W[colour, j, 6] = diagonal
                W[colour, j, 7] = 1.0 / diagonal
            return carry

        lax.fori_loop(0, EDGE, prepare, 0)

        for sweep in range(SWEEPS):
            for colour in range(2):
                last = sweep == SWEEPS - 1 and colour == 1

                def update(j, carry, colour=colour, last=last):
                    weights = [W[colour, j, k] for k in range(8)]
                    for c in range(3):
                        summed = total(s, colour, c, j, weights)
                        new = summed * weights[7]
                        U[s, colour, c, j + 1] = new
                        if last:
                            RB[c, j] = summed - weights[6] * new
                    return carry

                lax.fori_loop(0, EDGE, update, 0)

        taken = RIM[s, 48:56]

        def finish(big, carry):
            tiles = [[], [], [], [], [], []]
            for small in range(4):
                j = 4 * big + small
                weights = [W[0, j, k] for k in range(7)]
                for c in range(3):
                    red, black = U[s, 0, c, j + 1], U[s, 1, c, j + 1]
                    left = total(s, 0, c, j, weights) - weights[6] * red
                    tiles[c].append(left + RB[c, j])
                    tiles[3 + c].append(red + black)
                    start = c * 1024 + 64 * j + s
                    fo[pl.ds(start, 8, stride=SLOTS), :] = jnp.where(even, red, black) * taken
                    fo[pl.ds(start + 32, 8, stride=SLOTS), :] = (
                        jnp.where(even, black, red) * taken
                    )
            even_z = (third & 1) == 0
            even_y = (quarter & 1) == 0
            for k in range(6):
                halves = []
                for h in range(2):
                    one, two = tiles[k][2 * h], tiles[k][2 * h + 1]
                    halves.append(
                        jnp.where(
                            even_z, one + pltpu.roll(one, 127, 1), two + pltpu.roll(two, 1, 1)
                        )
                    )
                MEAN[s, k, big] = 0.125 * jnp.where(
                    even_y,
                    halves[0] + pltpu.roll(halves[0], 96, 1),
                    halves[1] + pltpu.roll(halves[1], 32, 1),
                )
            return carry

        lax.fori_loop(0, 4, finish, 0)

        @pl.when(turn < peers)
        def _():
            push(
                MEAN.at[s], RET.at[me], csend.at[turn - 1], crecv.at[turn - 1], {"gx": s}
            ).start()

        return carry

    lax.fori_loop(1, peers + 1, one_slot, 0)
    RET[me] = MEAN[me]

    for turn in range(1, peers):
        owner_at = lax.rem(me + turn, peers)
        push(
            MEAN.at[owner_at], RET.at[owner_at], csend.at[turn - 1], crecv.at[turn - 1], beside(0, 1)
        ).wait_recv()

    first_here = (lane >> 4) == positions[0]
    second_here = (lane >> 4) == positions[1]

    def spread(big, carry):
        for k in range(6):
            first = RET[groups[0], k, big]
            second = RET[groups[1], k, big]
            for small in range(4):
                x = 4 * big + small
                for h in range(2):
                    index = (2 * h + (small >> 1)) * 32 + (small & 1) + 2 * (lane & 15)
                    rows = pl.ds(h, 8, stride=2)
                    base = C[k - 3, x + 1, rows, :] if k >= 3 else jnp.zeros(TILE, jnp.float32)
                    value = jnp.where(
                        first_here,
                        lane_take(first, index),
                        jnp.where(second_here, lane_take(second, index), base),
                    )
                    if k >= 3:
                        SP[k - 3, x + 1, rows, :] = value
                        so[k - 3, x, rows, :] = value
                    else:
                        RM[k, x, rows, :] = value
        return carry

    lax.fori_loop(0, 4, spread, 0)

    outward2 = faces(SP, pl.ds(1, EDGE), HX2, HY2, HZ2, ZF2, dsend, drecv)
    for copy in outward2[:4]:
        copy.start()
    packed = jnp.zeros(SLAB, jnp.float32)
    for c in range(3):
        for x in range(EDGE):
            plane = SP[c, x + 1]
            low, high = 32 * c + x, 32 * c + 16 + x
            packed = jnp.where(lane16 == low, pltpu.roll(plane, (low - 127) % 128, 1), packed)
            packed = jnp.where(lane16 == high, pltpu.roll(plane, high, 1), packed)
    ZF2[...] = packed
    for copy in outward2[4:]:
        copy.start()

    for facing in range(2):
        for c in range(4):
            C[c, facing * 17] = HX[facing, c]
    loads[5].wait()
    for copy in outward2:
        copy.wait_recv()
    for facing in range(2):
        outside = at[0] == (size[0] - 1 if facing else 0)
        SP[:, facing * 17] = jnp.where(outside, 0.0, HX2[facing])
        outside = at[1] == (size[1] - 1 if facing else 0)
        HY2[facing] = jnp.where(outside, 0.0, HY2[facing])
        outside = at[2] == (size[2] - 1 if facing else 0)
        HZ2[facing] = jnp.where(outside, 0.0, HZ2[facing])

    refined_here = (group16 == positions[0]) | (group16 == positions[1])

    def leftover(x, carry):
        def neighbours(block, c, hy, hz):
            centre = block[c, x + 1]
            lanes = [
                lane_take(hz[f], jnp.full(SLAB, 32 * c + 16 * f, jnp.int32) + x) for f in range(2)
            ]
            rows = [jnp.broadcast_to(hy[f, c, pl.ds(x, 1), :], SLAB) for f in range(2)]
            return centre, [
                block[c, x],
                block[c, x + 2],
                jnp.where(row16 == 0, rows[0], pltpu.roll(centre, 1, 0)),
                jnp.where(row16 == 15, rows[1], pltpu.roll(centre, 15, 0)),
                jnp.where(lane16 == 0, lanes[0], pltpu.roll(centre, 1, 1)),
                jnp.where(lane16 == 127, lanes[1], pltpu.roll(centre, 127, 1)),
            ]

        centre, near = neighbours(C, 3, HY, HZ)
        face = [0.5 * (centre + value) for value in near]
        for c in range(3):
            centre, near = neighbours(SP, c, HY2, HZ2)
            applied = face[0] * (centre - near[0])
            for k in range(1, 6):
                applied = applied + face[k] * (centre - near[k])
            left = CR[c, x] - (REACTION * centre + 0.25 * applied)
            ro[c, x] = jnp.where(refined_here, RM[c, x], left)
        return carry

    lax.fori_loop(0, EDGE, leftover, 0)

    for copy in outward + out_rims + outward2:
        copy.wait_send()
    for turn in range(1, peers):
        owner_at = lax.rem(me + turn, peers)
        push(
            MEAN.at[owner_at], RET.at[owner_at], csend.at[turn - 1], crecv.at[turn - 1], beside(0, 1)
        ).wait_send()


def shards(cv, cm, cr, fv, fr, fm, refined, owner):
    def rows_of(values):
        return values[0].transpose(1, 0, 2).reshape(3, SLOTS, 256, 128).transpose(
            0, 2, 1, 3
        ).reshape(3072, 128)

    f32 = jnp.float32
    vmem = lambda *shape: pltpu.VMEM(shape, f32)
    dma = lambda count: pltpu.SemaphoreType.DMA((count,))
    any_space = pl.BlockSpec(memory_space=pl.ANY)
    in_vmem = pl.BlockSpec(memory_space=pltpu.VMEM)
    in_smem = pl.BlockSpec(memory_space=pltpu.SMEM)
    shape = jax.ShapeDtypeStruct
    fine, synced, residual = pl.pallas_call(
        kernel,
        name="smooth",
        out_shape=[
            shape((3072, 128), f32),
            shape((3, 16, 16, 128), f32),
            shape((3, 16, 16, 128), f32),
        ],
        in_specs=[any_space] * 6 + [in_smem] * 2,
        out_specs=[in_vmem] * 3,
        scratch_shapes=[
            vmem(4, 18, 16, 128),
            vmem(3, 16, 16, 128),
            vmem(3072, 128),
            vmem(3072, 128),
            vmem(1024, 128),
            vmem(2, 4, 16, 128),
            vmem(2, 4, 16, 128),
            vmem(2, 16, 128),
            vmem(2, 4, 16, 128),
            vmem(16, 128),
            vmem(4, 56, 128),
            vmem(4, 56, 128),
            vmem(4, 2, 18, 8, 128),
            vmem(4, 2, 3, 18, 8, 128),
            vmem(4, 2, 3, 16, 8, 128),
            vmem(2, 16, 8, 8, 128),
            vmem(4, 16, 128),
            vmem(3, 16, 8, 128),
            vmem(4, 6, 4, 8, 128),
            vmem(4, 6, 4, 8, 128),
            vmem(3, 18, 16, 128),
            vmem(3, 16, 16, 128),
            vmem(2, 3, 16, 128),
            vmem(2, 3, 16, 128),
            vmem(2, 16, 128),
            vmem(16, 128),
            dma(6), dma(6), dma(6), dma(3), dma(3), dma(3), dma(3), dma(6), dma(6),
        ],
        compiler_params=pltpu.CompilerParams(
            collective_id=0, has_side_effects=True, vmem_limit_bytes=48 * 2**20
        ),
    )(
        cv, cm, cr, rows_of(fv), rows_of(fr),
        fm[0].reshape(SLOTS, 256, 128).transpose(1, 0, 2).reshape(1024, 128),
        refined, owner,
    )
    fine = fine.reshape(3, 256, SLOTS, 128).transpose(0, 2, 1, 3).reshape(3, SLOTS, 32768)
    return fine.transpose(1, 0, 2)[None], synced, residual


def solution(mesh):
    block = P(None, "gx", "gy", "gz")
    slots = P(("gx", "gy", "gz"))
    return jax.shard_map(
        shards,
        mesh=mesh,
        in_specs=(block, P("gx", "gy", "gz"), block, slots, slots, slots, slots, slots),
        out_specs=(slots, block, block),
        check_vma=False,
    )
```

```python
import functools

import jax
import jax.numpy as jnp
from jax import lax
from jax.experimental import pallas as pl
from jax.experimental.pallas import tpu as pltpu
from jax.sharding import PartitionSpec as P

SWEEPS = 2
EDGE = 16
SLOTS = 4
GROUP = 16
REACTION = 1.0
TILE = (8, 128)
SLAB = (16, 128)
MESH = pl.DeviceIdType.MESH
AXES = ("gx", "gy", "gz")


def lane_take(values, index):
    numbers = lax.GatherDimensionNumbers(
        offset_dims=(),
        collapsed_slice_dims=(1,),
        start_index_map=(1,),
        operand_batching_dims=(0,),
        start_indices_batching_dims=(0,),
    )
    return lax.gather(
        values,
        index[..., None],
        numbers,
        slice_sizes=(1, 1),
        mode=lax.GatherScatterMode.PROMISE_IN_BOUNDS,
    )


def push(source, target, sent, landed, device):
    return pltpu.make_async_remote_copy(
        src_ref=source,
        dst_ref=target,
        send_sem=sent,
        recv_sem=landed,
        device_id=device,
        device_id_type=MESH,
    )


def kernel(
    cv, cm, cr, fv, fr, fm, place_in, own_in,
    fo, C, CR, HY, HZ, SP, RM, HY2, HZ2, mask,
    FV, FR, FM, HX, EF, ZF, MSG, RIM, PV, U, LD, W, GY, RB,
    MEAN, RET, HX2, ZF2, place, own,
    lsem, asend, arecv, bsend, brecv, csend, crecv, dsend, drecv,
):
    at = [lax.axis_index(axis) for axis in AXES]
    size = [lax.axis_size(axis) for axis in AXES]
    me, peers = at[0], size[0]

    def beside(number, step):
        return {AXES[number]: lax.rem(at[number] + (step + size[number]), size[number])}

    loads = [
        pltpu.make_async_copy(cv, C.at[0:3, 1 : EDGE + 1], lsem.at[0]),
        pltpu.make_async_copy(cm, C.at[3, 1 : EDGE + 1], lsem.at[1]),
        pltpu.make_async_copy(fm, FM, lsem.at[2]),
        pltpu.make_async_copy(fr, FR, lsem.at[3]),
        pltpu.make_async_copy(fv, FV, lsem.at[4]),
        pltpu.make_async_copy(cr, CR, lsem.at[5]),
        pltpu.make_async_copy(place_in, place, lsem.at[6]),
        pltpu.make_async_copy(own_in, own, lsem.at[7]),
    ]
    for load in loads:
        load.start()

    barrier = pltpu.get_barrier_semaphore()
    for step in range(1, peers):
        pl.semaphore_signal(barrier, inc=1, device_id=beside(0, step), device_id_type=MESH)
    for number in (1, 2):
        for step in (1, -1):
            pl.semaphore_signal(
                barrier, inc=1, device_id=beside(number, step), device_id_type=MESH
            )
    lane = lax.broadcasted_iota(jnp.int32, TILE, 1)
    row = lax.broadcasted_iota(jnp.int32, TILE, 0)
    third = lane & 31
    quarter = lane >> 5
    even = ((third + quarter) & 1) == 0
    z_first, z_last = third == 0, third == 31
    y_first = (row == 0) & (quarter == 0)
    y_last = (row == 7) & (quarter == 3)
    lane16 = lax.broadcasted_iota(jnp.int32, SLAB, 1)
    row16 = lax.broadcasted_iota(jnp.int32, SLAB, 0)
    group16 = lane16 >> 4
    inner16 = lane16 & 15

    def faces(block, planes, hx, hy, hz, packed, sent, landed):
        first, last = 1, EDGE
        return [
            push(block.at[:, last], hx.at[0], sent.at[0], landed.at[0], beside(0, 1)),
            push(block.at[:, first], hx.at[1], sent.at[1], landed.at[1], beside(0, -1)),
            push(block.at[:, planes, EDGE - 1], hy.at[0], sent.at[2], landed.at[2], beside(1, 1)),
            push(block.at[:, planes, 0], hy.at[1], sent.at[3], landed.at[3], beside(1, -1)),
            push(packed, hz.at[0], sent.at[4], landed.at[4], beside(2, 1)),
            push(packed, hz.at[1], sent.at[5], landed.at[5], beside(2, -1)),
        ]

    loads[0].wait()
    loads[1].wait()
    packed = jnp.zeros(SLAB, jnp.float32)
    for c in range(4):
        upper = jnp.zeros(SLAB, jnp.float32)
        lower = jnp.zeros(SLAB, jnp.float32)
        for x in range(EDGE):
            plane = C[c, x + 1]
            here = inner16 == x
            upper = jnp.where(here, pltpu.roll(plane, (x - 15) % 128, 1), upper)
            lower = jnp.where(here, pltpu.roll(plane, x, 1), lower)
        EF[0, c] = upper
        EF[1, c] = lower
        turn = (32 * c + 16) % 128
        packed = jnp.where(group16 == 2 * c, pltpu.roll(upper, turn, 1), packed)
        packed = jnp.where(group16 == 2 * c + 1, pltpu.roll(lower, turn, 1), packed)
    ZF[...] = packed
    pl.semaphore_wait(barrier, peers + 3)
    outward = faces(C, pl.ds(1, EDGE), HX, HY, HZ, ZF, asend, arecv)
    for copy in outward:
        copy.start()

    loads[2].wait()
    loads[3].wait()
    loads[4].wait()

    def pack(j, carry):
        def pair(ref, start):
            low = ref[pl.ds(start + 64 * j, 8, stride=SLOTS), :]
            high = ref[pl.ds(start + 64 * j + 32, 8, stride=SLOTS), :]
            return jnp.where(even, low, high), jnp.where(even, high, low)

        for s in range(SLOTS):
            PV[s, 0, j + 1], PV[s, 1, j + 1] = pair(FM, s)
            for c in range(3):
                LD[s, 0, c, j], LD[s, 1, c, j] = pair(FR, c * 1024 + s)
                U[s, 0, c, j + 1], U[s, 1, c, j + 1] = pair(FV, c * 1024 + s)
        return carry

    def y_up(tile):
        turned = pltpu.roll(tile, 96, 1)
        return jnp.where(quarter == 3, pltpu.roll(turned, 7, 0), turned)

    def y_down(tile):
        turned = pltpu.roll(tile, 32, 1)
        return jnp.where(quarter == 0, pltpu.roll(turned, 1, 0), turned)

    def far(colour, before, after):
        if colour == 0:
            return jnp.where(even, before, after)
        return jnp.where(even, after, before)

    def prepare(step, carry):
        s, big = step >> 2, step & 3
        stores = []
        for small in range(4):
            j = 4 * big + small
            for colour in range(2):
                own_tile = PV[s, colour, j + 1]
                other = PV.at[s, 1 - colour]
                tile = other[j + 1]
                face = [
                    0.5 * (own_tile + value)
                    for value in (
                        tile,
                        far(colour, other[j], other[j + 2]),
                        jnp.where(y_first, 0.0, y_down(tile)),
                        jnp.where(y_last, 0.0, y_up(tile)),
                        jnp.where(z_first, 0.0, pltpu.roll(tile, 1, 1)),
                        jnp.where(z_last, 0.0, pltpu.roll(tile, 127, 1)),
                    )
                ]
                diagonal = REACTION + face[0]
                for value in face[1:]:
                    diagonal = diagonal + value
                inside = face[:2] + [
                    jnp.where(outer, 0.0, value)
                    for outer, value in zip((y_first, y_last, z_first, z_last), face[2:])
                ]
                stores.append((colour, j, inside + [diagonal]))
        for colour, j, values in stores:
            for k, value in enumerate(values):
                W[s, colour, j, k] = value
        return carry

    for s in range(SLOTS):
        for colour in range(2):
            for end in (0, EDGE + 1):
                PV[s, colour, end] = jnp.zeros(TILE, jnp.float32)
    lax.fori_loop(0, EDGE, pack, 0)
    lax.fori_loop(0, EDGE, prepare, 0)

    for copy in outward:
        copy.wait_recv()
    for number, halo in ((0, HX), (1, HY)):
        for facing in range(2):
            outside = at[number] == (size[number] - 1 if facing else 0)
            halo[facing] = jnp.where(outside, 0.0, halo[facing])
    for facing in range(2):
        outside = at[2] == (size[2] - 1 if facing else 0)
        HZ[facing] = jnp.where(outside, 0.0, HZ[facing])

    loads[6].wait()
    loads[7].wait()
    positions = [place[0, 0], place[0, 1]]
    groups = [lax.div(own[0, i], size[1] * size[2]) for i in range(2)]
    odd_group = (group16 & 1) == 1
    across = jnp.where(odd_group, HZ[1], HZ[0])
    rims = []
    for i in range(2):
        p = positions[i]
        parts = [jnp.zeros(SLAB, jnp.float32)] * 3
        for c in range(4):
            for facing in range(2):
                g = 2 * c + facing
                here = group16 == g
                turn = (16 * g - 16 * p) & 127
                turn_z = (16 * g - 16 * p + (-16 if facing else 16)) & 127
                parts = [
                    jnp.where(here, pltpu.roll(HX[facing, c], turn, 1), parts[0]),
                    jnp.where(here, pltpu.roll(HY[facing, c], turn, 1), parts[1]),
                    jnp.where(here, pltpu.roll(EF[facing, c], turn_z, 1), parts[2]),
                ]
        parts[2] = jnp.where(jnp.where(odd_group, p - 7, p) == 0, across, parts[2])
        rims.append(parts)
    for peer in range(peers):
        is_first = jnp.full(SLAB, groups[0], jnp.int32) == peer
        for k in range(3):
            MSG[peer, 16 * k : 16 * k + 16] = jnp.where(is_first, rims[0][k], rims[1][k])
        first = jnp.full(TILE, groups[0], jnp.int32) == peer
        second = jnp.full(TILE, groups[1], jnp.int32) == peer
        MSG[peer, 48:56] = jnp.where(first | second, 1.0, 0.0)
    out_rims = []
    for step in range(1, peers):
        peer = lax.rem(me + step, peers)
        out_rims.append(
            push(
                MSG.at[peer], RIM.at[me], bsend.at[step - 1], brecv.at[step - 1], beside(0, step)
            )
        )
        out_rims[-1].start()
    RIM[me] = MSG[me]

    def total(s, colour, c, j, weights):
        other = U.at[s, 1 - colour, c]
        tile = other[j + 1]
        return (
            LD[s, colour, c, j]
            + weights[0] * tile
            + weights[1] * far(colour, other[j], other[j + 2])
            + weights[2] * y_down(tile)
            + weights[3] * y_up(tile)
            + weights[4] * pltpu.roll(tile, 1, 1)
            + weights[5] * pltpu.roll(tile, 127, 1)
        )

    def one_slot(turn, carry):
        s = lax.rem(me + (2 * peers - turn), peers)

        @pl.when(turn < peers)
        def _():
            push(
                MSG.at[s], RIM.at[s], bsend.at[turn - 1], brecv.at[turn - 1], beside(0, 1)
            ).wait_recv()

        high_half = quarter >= 2
        x_rows = [RIM[s, pl.ds(h, 8, stride=2), :] for h in range(2)]
        z_rows = [RIM[s, pl.ds(32 + h, 8, stride=2), :] for h in range(2)]
        y_slab = RIM[s, 16:32]
        rim_x = []
        for c in range(4):
            for facing in range(2):
                index = 16 * (2 * c + facing) + (third >> 1)
                ghost = jnp.where(
                    high_half, lane_take(x_rows[1], index), lane_take(x_rows[0], index)
                )
                if c == 3:
                    rim_x.append(ghost)
                else:
                    for colour in range(2):
                        U[s, colour, c, facing * 17] = ghost
            index = 32 * c + jnp.where((lane16 >> 5) == 3, 16, 0) + ((lane16 & 31) >> 1)
            GY[c] = lane_take(y_slab, index)
        for colour in range(2):
            for facing in range(2):
                j = (EDGE - 1) * facing
                at_rim = even if colour == facing else jnp.logical_not(even)
                more = jnp.where(at_rim, 0.5 * rim_x[facing], 0.0)
                W[s, colour, j, 1] = W[s, colour, j, 1] + more
                W[s, colour, j, 6] = W[s, colour, j, 6] + more

        at_z = z_first | z_last
        at_y = y_first | y_last

        def surround(big, carry):
            stores = []
            for small in range(4):
                j = 4 * big + small
                ghost_z, ghost_y = [], []
                for c in range(4):
                    index = 32 * c + j + jnp.where(z_last, 16, 0)
                    ghost_z.append(
                        jnp.where(
                            high_half, lane_take(z_rows[1], index), lane_take(z_rows[0], index)
                        )
                    )
                    ghost_y.append(jnp.broadcast_to(GY[c, pl.ds(j, 1), :], TILE))
                for colour in range(2):
                    half = 0.5 * PV[s, colour, j + 1]
                    half_z, half_y = 0.5 * ghost_z[3], 0.5 * ghost_y[3]
                    rim_z = jnp.where(at_z, half + half_z, 0.0)
                    rim_y = jnp.where(at_y, half + half_y, 0.0)
                    diagonal = (
                        W[s, colour, j, 6]
                        + jnp.where(at_z, half_z, 0.0)
                        + jnp.where(at_y, half_y, 0.0)
                    )
                    loaded = [
                        LD[s, colour, c, j] + rim_y * ghost_y[c] + rim_z * ghost_z[c]
                        for c in range(3)
                    ]
                    stores.append((colour, j, diagonal, 1.0 / diagonal, loaded))
            for colour, j, diagonal, inverse, loaded in stores:
                W[s, colour, j, 6] = diagonal
                W[s, colour, j, 7] = inverse
                for c in range(3):
                    LD[s, colour, c, j] = loaded[c]
            return carry

        lax.fori_loop(0, 4, surround, 0)

        for sweep in range(SWEEPS):
            for colour in range(2):
                last = sweep == SWEEPS - 1 and colour == 1

                def update(big, carry, colour=colour, last=last):
                    stores = []
                    for small in range(GROUP):
                        j = GROUP * big + small
                        weights = [W[s, colour, j, k] for k in range(8)]
                        for c in range(3):
                            summed = total(s, colour, c, j, weights)
                            new = summed * weights[7]
                            left = summed - weights[6] * new if last else None
                            stores.append((c, j, new, left))
                    for c, j, new, left in stores:
                        U[s, colour, c, j + 1] = new
                        if last:
                            RB[c, j] = left
                    return carry

                lax.fori_loop(0, EDGE // GROUP, update, 0)

        taken = RIM[s, 48:56]

        def finish(big, carry):
            tiles = [[], [], [], [], [], []]
            stores = []
            for small in range(4):
                j = 4 * big + small
                weights = [W[s, 0, j, k] for k in range(7)]
                for c in range(3):
                    red, black = U[s, 0, c, j + 1], U[s, 1, c, j + 1]
                    left = total(s, 0, c, j, weights) - weights[6] * red
                    tiles[c].append(left + RB[c, j])
                    tiles[3 + c].append(red + black)
                    start = c * 1024 + 64 * j + s
                    stores.append((start, jnp.where(even, red, black) * taken))
                    stores.append((start + 32, jnp.where(even, black, red) * taken))
            even_z = (third & 1) == 0
            even_y = (quarter & 1) == 0
            means = []
            for k in range(6):
                halves = []
                for h in range(2):
                    one, two = tiles[k][2 * h], tiles[k][2 * h + 1]
                    halves.append(
                        jnp.where(
                            even_z, one + pltpu.roll(one, 127, 1), two + pltpu.roll(two, 1, 1)
                        )
                    )
                means.append(
                    0.125
                    * jnp.where(
                        even_y,
                        halves[0] + pltpu.roll(halves[0], 96, 1),
                        halves[1] + pltpu.roll(halves[1], 32, 1),
                    )
                )
            for k in range(6):
                MEAN[s, k, big] = means[k]
            for start, tile in stores:
                fo[pl.ds(start, 8, stride=SLOTS), :] = tile
            return carry

        lax.fori_loop(0, 4, finish, 0)

        @pl.when(turn < peers)
        def _():
            push(
                MEAN.at[s], RET.at[me], csend.at[turn - 1], crecv.at[turn - 1], {"gx": s}
            ).start()

        return carry

    lax.fori_loop(1, peers + 1, one_slot, 0)
    RET[me] = MEAN[me]

    for turn in range(1, peers):
        owner_at = lax.rem(me + turn, peers)
        push(
            MEAN.at[owner_at], RET.at[owner_at], csend.at[turn - 1], crecv.at[turn - 1], beside(0, 1)
        ).wait_recv()

    first_here = (lane >> 4) == positions[0]
    second_here = (lane >> 4) == positions[1]

    def spread(big, carry):
        stores = []
        for k in range(6):
            first = RET[groups[0], k, big]
            second = RET[groups[1], k, big]
            for small in range(4):
                x = 4 * big + small
                for h in range(2):
                    index = (2 * h + (small >> 1)) * 32 + (small & 1) + 2 * (lane & 15)
                    rows = pl.ds(h, 8, stride=2)
                    base = C[k - 3, x + 1, rows, :] if k >= 3 else jnp.zeros(TILE, jnp.float32)
                    value = jnp.where(
                        first_here,
                        lane_take(first, index),
                        jnp.where(second_here, lane_take(second, index), base),
                    )
                    stores.append((k, x, rows, value))
        for k, x, rows, value in stores:
            if k >= 3:
                SP[k - 3, x + 1, rows, :] = value
            else:
                RM[k, x, rows, :] = value
        return carry

    lax.fori_loop(0, 4, spread, 0)

    outward2 = faces(SP, pl.ds(1, EDGE), HX2, HY2, HZ2, ZF2, dsend, drecv)
    for copy in outward2[:4]:
        copy.start()
    packed = jnp.zeros(SLAB, jnp.float32)
    for c in range(3):
        for x in range(EDGE):
            plane = SP[c, x + 1]
            low, high = 32 * c + x, 32 * c + 16 + x
            packed = jnp.where(lane16 == low, pltpu.roll(plane, (low - 127) % 128, 1), packed)
            packed = jnp.where(lane16 == high, pltpu.roll(plane, high, 1), packed)
    ZF2[...] = packed
    for copy in outward2[4:]:
        copy.start()

    for facing in range(2):
        for c in range(4):
            C[c, facing * 17] = HX[facing, c]
    loads[5].wait()
    for copy in outward2:
        copy.wait_recv()
    for facing in range(2):
        outside = at[0] == (size[0] - 1 if facing else 0)
        SP[:, facing * 17] = jnp.where(outside, 0.0, HX2[facing])
        outside = at[1] == (size[1] - 1 if facing else 0)
        HY2[facing] = jnp.where(outside, 0.0, HY2[facing])
        outside = at[2] == (size[2] - 1 if facing else 0)
        HZ2[facing] = jnp.where(outside, 0.0, HZ2[facing])

    refined_here = (group16 == positions[0]) | (group16 == positions[1])
    mask[...] = jnp.where(refined_here, 1.0, 0.0)
    for copy in outward + out_rims + outward2:
        copy.wait_send()
    for turn in range(1, peers):
        owner_at = lax.rem(me + turn, peers)
        push(
            MEAN.at[owner_at], RET.at[owner_at], csend.at[turn - 1], crecv.at[turn - 1], beside(0, 1)
        ).wait_send()


def write_out(
    fine, C, CR, HY, HZ, SP, RM, HY2, HZ2, mask, fo, so, ro, R, sem
):
    copies = [
        pltpu.make_async_copy(SP.at[:, 1 : EDGE + 1], so, sem.at[0]),
        pltpu.make_async_copy(fine, fo, sem.at[1]),
        pltpu.make_async_copy(R, ro, sem.at[2]),
    ]
    copies[0].start()
    copies[1].start()
    lane16 = lax.broadcasted_iota(jnp.int32, SLAB, 1)
    row16 = lax.broadcasted_iota(jnp.int32, SLAB, 0)
    refined_here = mask[...] > 0.5

    def leftover(big, carry):
        def neighbours(block, c, x, hy, hz):
            centre = block[c, x + 1]
            lanes = [
                lane_take(hz[f], jnp.full(SLAB, 32 * c + 16 * f, jnp.int32) + x) for f in range(2)
            ]
            rows = [jnp.broadcast_to(hy[f, c, pl.ds(x, 1), :], SLAB) for f in range(2)]
            return centre, [
                block[c, x],
                block[c, x + 2],
                jnp.where(row16 == 0, rows[0], pltpu.roll(centre, 1, 0)),
                jnp.where(row16 == 15, rows[1], pltpu.roll(centre, 15, 0)),
                jnp.where(lane16 == 0, lanes[0], pltpu.roll(centre, 1, 1)),
                jnp.where(lane16 == 127, lanes[1], pltpu.roll(centre, 127, 1)),
            ]

        stores = []
        for small in range(2):
            x = 2 * big + small
            centre, near = neighbours(C, 3, x, HY, HZ)
            face = [0.5 * (centre + value) for value in near]
            for c in range(3):
                centre, near = neighbours(SP, c, x, HY2, HZ2)
                applied = face[0] * (centre - near[0])
                for k in range(1, 6):
                    applied = applied + face[k] * (centre - near[k])
                left = CR[c, x] - (REACTION * centre + 0.25 * applied)
                stores.append((c, x, jnp.where(refined_here, RM[c, x], left)))
        for c, x, left in stores:
            R[c, x] = left
        return carry

    lax.fori_loop(0, EDGE // 2, leftover, 0)
    copies[2].start()
    for copy in copies:
        copy.wait()


def shards(cv, cm, cr, fv, fr, fm, refined, owner):
    def rows_of(values):
        return values[0].transpose(1, 0, 2).reshape(3, SLOTS, 256, 128).transpose(
            0, 2, 1, 3
        ).reshape(3072, 128)

    f32 = jnp.float32
    vmem = lambda *shape: pltpu.VMEM(shape, f32)
    dma = lambda count: pltpu.SemaphoreType.DMA((count,))
    any_space = pl.BlockSpec(memory_space=pltpu.HBM)
    in_vmem = pl.BlockSpec(memory_space=pltpu.VMEM)
    shape = jax.ShapeDtypeStruct
    here = lambda x: pltpu.with_memory_space_constraint(x, pltpu.HBM)
    kept = [
        (3072, 128),
        (4, 18, 16, 128),
        (3, 16, 16, 128),
        (2, 4, 16, 128),
        (2, 16, 128),
        (3, 18, 16, 128),
        (3, 16, 16, 128),
        (2, 3, 16, 128),
        (2, 16, 128),
        (16, 128),
    ]
    held = pl.pallas_call(
        kernel,
        name="smooth",
        out_shape=[vmem(*dims) for dims in kept],
        in_specs=[any_space] * 8,
        out_specs=[in_vmem] * len(kept),
        scratch_shapes=[
            vmem(3072, 128),
            vmem(3072, 128),
            vmem(1024, 128),
            vmem(2, 4, 16, 128),
            vmem(2, 4, 16, 128),
            vmem(16, 128),
            vmem(4, 56, 128),
            vmem(4, 56, 128),
            vmem(4, 2, 18, 8, 128),
            vmem(4, 2, 3, 18, 8, 128),
            vmem(4, 2, 3, 16, 8, 128),
            vmem(4, 2, 16, 8, 8, 128),
            vmem(4, 16, 128),
            vmem(3, 16, 8, 128),
            vmem(4, 6, 4, 8, 128),
            vmem(4, 6, 4, 8, 128),
            vmem(2, 3, 16, 128),
            vmem(16, 128),
            pltpu.SMEM((1, 2), jnp.int32),
            pltpu.SMEM((1, 2), jnp.int32),
            dma(8), dma(6), dma(6), dma(3), dma(3), dma(3), dma(3), dma(6), dma(6),
        ],
        compiler_params=pltpu.CompilerParams(
            collective_id=0, has_side_effects=True, vmem_limit_bytes=48 * 2**20
        ),
    )(
        here(cv), here(cm), here(cr), here(rows_of(fv)), here(rows_of(fr)),
        here(fm[0].reshape(SLOTS, 256, 128).transpose(1, 0, 2).reshape(1024, 128)),
        here(refined), here(owner),
    )
    fine, synced, residual = pl.pallas_call(
        write_out,
        name="write_out",
        out_shape=[
            shape((3072, 128), f32),
            shape((3, 16, 16, 128), f32),
            shape((3, 16, 16, 128), f32),
        ],
        in_specs=[in_vmem] * len(kept),
        out_specs=[any_space] * 3,
        scratch_shapes=[vmem(3, 16, 16, 128), dma(3)],
    )(*(pltpu.with_memory_space_constraint(x, pltpu.VMEM) for x in held))
    fine = fine.reshape(3, 256, SLOTS, 128).transpose(0, 2, 1, 3).reshape(3, SLOTS, 32768)
    return fine.transpose(1, 0, 2)[None], synced, residual


def solution(mesh):
    block = P(None, "gx", "gy", "gz")
    slots = P(("gx", "gy", "gz"))
    return jax.shard_map(
        shards,
        mesh=mesh,
        in_specs=(block, P("gx", "gy", "gz"), block, slots, slots, slots, slots, slots),
        out_specs=(slots, block, block),
        check_vma=False,
    )
```

```python
import functools

import jax
import jax.numpy as jnp
from jax import lax
from jax.experimental import pallas as pl
from jax.experimental.pallas import tpu as pltpu
from jax.sharding import PartitionSpec as P

SWEEPS = 2
EDGE = 16
SLOTS = 4
REACTION = 1.0
TILE = (8, 128)
SLAB = (16, 128)
MESH = pl.DeviceIdType.MESH
AXES = ("gx", "gy", "gz")


def lane_take(values, index):
    numbers = lax.GatherDimensionNumbers(
        offset_dims=(),
        collapsed_slice_dims=(1,),
        start_index_map=(1,),
        operand_batching_dims=(0,),
        start_indices_batching_dims=(0,),
    )
    return lax.gather(
        values,
        index[..., None],
        numbers,
        slice_sizes=(1, 1),
        mode=lax.GatherScatterMode.PROMISE_IN_BOUNDS,
    )


def push(source, target, sent, landed, device):
    return pltpu.make_async_remote_copy(
        src_ref=source,
        dst_ref=target,
        send_sem=sent,
        recv_sem=landed,
        device_id=device,
        device_id_type=MESH,
    )


def kernel(
    cv, cm, cr, fv, fr, fm, place_in, own_in,
    fo, C, CR, HX, HY, HZ, RX, RY, RZ, RS, M,
    FV, FR, FM, EF, ZF, MSG, RIM, PV, U, LD, W, GY, RB,
    MEAN, RET, ZM, place, own,
    lsem, asend, arecv, bsend, brecv, csend, crecv, dsend, drecv,
):
    at = [lax.axis_index(axis) for axis in AXES]
    size = [lax.axis_size(axis) for axis in AXES]
    me, peers = at[0], size[0]

    def beside(number, step):
        return {AXES[number]: lax.rem(at[number] + (step + size[number]), size[number])}

    loads = [
        pltpu.make_async_copy(cv, C.at[0:3, 1 : EDGE + 1], lsem.at[0]),
        pltpu.make_async_copy(cm, C.at[3, 1 : EDGE + 1], lsem.at[1]),
        pltpu.make_async_copy(fm, FM, lsem.at[2]),
        pltpu.make_async_copy(fr, FR, lsem.at[3]),
        pltpu.make_async_copy(fv, FV, lsem.at[4]),
        pltpu.make_async_copy(cr, CR, lsem.at[5]),
        pltpu.make_async_copy(place_in, place, lsem.at[6]),
        pltpu.make_async_copy(own_in, own, lsem.at[7]),
    ]
    for number in (6, 7, 0, 1, 2, 3, 4, 5):
        loads[number].start()

    barrier = pltpu.get_barrier_semaphore()
    for step in range(1, peers):
        pl.semaphore_signal(barrier, inc=1, device_id=beside(0, step), device_id_type=MESH)
    for number in (1, 2):
        for step in (1, -1):
            pl.semaphore_signal(
                barrier, inc=1, device_id=beside(number, step), device_id_type=MESH
            )
    lane = lax.broadcasted_iota(jnp.int32, TILE, 1)
    row = lax.broadcasted_iota(jnp.int32, TILE, 0)
    third = lane & 31
    quarter = lane >> 5
    even = ((third + quarter) & 1) == 0
    z_first, z_last = third == 0, third == 31
    y_first = (row == 0) & (quarter == 0)
    y_last = (row == 7) & (quarter == 3)
    lane16 = lax.broadcasted_iota(jnp.int32, SLAB, 1)
    row16 = lax.broadcasted_iota(jnp.int32, SLAB, 0)
    group16 = lane16 >> 4
    inner16 = lane16 & 15

    loads[6].wait()
    loads[7].wait()
    positions = [place[0, 0], place[0, 1]]
    groups = [lax.div(own[0, i], size[1] * size[2]) for i in range(2)]
    marks = [(groups[i] + 1).astype(jnp.float32) for i in range(2)]

    def marked(numbers, wanted):
        return jnp.where(
            numbers[0] == wanted, marks[0], jnp.where(numbers[1] == wanted, marks[1], 0.0)
        )

    spots = [jnp.full(SLAB, positions[i], jnp.int32) for i in range(2)]
    mark = marked(spots, group16)
    for x in range(EDGE):
        C[4, x + 1] = mark
    ZF[16:32] = jnp.where((group16 & 1) == 1, marked(spots, 0), marked(spots, 7))
    for i in range(2):
        M[i] = jnp.where(group16 == positions[i], 1.0, 0.0)

    loads[0].wait()
    loads[1].wait()
    packed = jnp.zeros(SLAB, jnp.float32)
    for c in range(4):
        upper = jnp.zeros(SLAB, jnp.float32)
        lower = jnp.zeros(SLAB, jnp.float32)
        for x in range(EDGE):
            plane = C[c, x + 1]
            here = inner16 == x
            upper = jnp.where(here, pltpu.roll(plane, (x - 15) % 128, 1), upper)
            lower = jnp.where(here, pltpu.roll(plane, x, 1), lower)
        EF[0, c] = upper
        EF[1, c] = lower
        turn = (32 * c + 16) % 128
        packed = jnp.where(group16 == 2 * c, pltpu.roll(upper, turn, 1), packed)
        packed = jnp.where(group16 == 2 * c + 1, pltpu.roll(lower, turn, 1), packed)
    ZF[0:16] = packed
    pl.semaphore_wait(barrier, peers + 3)
    inner = pl.ds(1, EDGE)
    outward = [
        push(C.at[:, EDGE], HX.at[0], asend.at[0], arecv.at[0], beside(0, 1)),
        push(C.at[:, 1], HX.at[1], asend.at[1], arecv.at[1], beside(0, -1)),
        push(C.at[:, inner, EDGE - 1], HY.at[0], asend.at[2], arecv.at[2], beside(1, 1)),
        push(C.at[:, inner, 0], HY.at[1], asend.at[3], arecv.at[3], beside(1, -1)),
        push(ZF, HZ.at[0], asend.at[4], arecv.at[4], beside(2, 1)),
        push(ZF, HZ.at[1], asend.at[5], arecv.at[5], beside(2, -1)),
    ]
    for copy in outward:
        copy.start()

    loads[2].wait()
    loads[3].wait()
    loads[4].wait()

    def pack(j, carry):
        def pair(ref, start):
            low = ref[pl.ds(start + 64 * j, 8, stride=SLOTS), :]
            high = ref[pl.ds(start + 64 * j + 32, 8, stride=SLOTS), :]
            return jnp.where(even, low, high), jnp.where(even, high, low)

        for s in range(SLOTS):
            slot = lax.rem(me + (peers - s), peers)
            PV[s, 0, j + 1], PV[s, 1, j + 1] = pair(FM, slot)
            for c in range(3):
                LD[s, 0, c, j], LD[s, 1, c, j] = pair(FR, c * 1024 + slot)
                U[s, 0, c, j + 1], U[s, 1, c, j + 1] = pair(FV, c * 1024 + slot)
        return carry

    def y_up(tile):
        turned = pltpu.roll(tile, 96, 1)
        return jnp.where(quarter == 3, pltpu.roll(turned, 7, 0), turned)

    def y_down(tile):
        turned = pltpu.roll(tile, 32, 1)
        return jnp.where(quarter == 0, pltpu.roll(turned, 1, 0), turned)

    def far(colour, before, after):
        if colour == 0:
            return jnp.where(even, before, after)
        return jnp.where(even, after, before)

    def prepare(step, carry):
        s, big = step >> 2, step & 3
        stores = []
        for small in range(4):
            j = 4 * big + small
            for colour in range(2):
                own_tile = PV[s, colour, j + 1]
                other = PV.at[s, 1 - colour]
                tile = other[j + 1]
                face = [
                    0.5 * (own_tile + value)
                    for value in (
                        tile,
                        far(colour, other[j], other[j + 2]),
                        jnp.where(y_first, 0.0, y_down(tile)),
                        jnp.where(y_last, 0.0, y_up(tile)),
                        jnp.where(z_first, 0.0, pltpu.roll(tile, 1, 1)),
                        jnp.where(z_last, 0.0, pltpu.roll(tile, 127, 1)),
                    )
                ]
                diagonal = REACTION + face[0]
                for value in face[1:]:
                    diagonal = diagonal + value
                inside = face[:2] + [
                    jnp.where(outer, 0.0, value)
                    for outer, value in zip((y_first, y_last, z_first, z_last), face[2:])
                ]
                stores.append((colour, j, inside + [diagonal]))
        for colour, j, values in stores:
            for k, value in enumerate(values):
                W[s, colour, j, k] = value
        return carry

    for s in range(SLOTS):
        for colour in range(2):
            for end in (0, EDGE + 1):
                PV[s, colour, end] = jnp.zeros(TILE, jnp.float32)
    lax.fori_loop(0, EDGE, pack, 0)
    lax.fori_loop(0, EDGE, prepare, 0)

    for copy in outward:
        copy.wait_recv()
    for number, halo in ((0, HX), (1, HY)):
        for facing in range(2):
            outside = at[number] == (size[number] - 1 if facing else 0)
            halo[facing] = jnp.where(outside, 0.0, halo[facing])
    for facing in range(2):
        outside = at[2] == (size[2] - 1 if facing else 0)
        HZ[facing] = jnp.where(outside, 0.0, HZ[facing])

    odd_group = (group16 & 1) == 1
    across = jnp.where(odd_group, HZ[1, 0:16], HZ[0, 0:16])
    rims = []
    for i in range(2):
        p = positions[i]
        parts = [jnp.zeros(SLAB, jnp.float32)] * 3
        for c in range(4):
            for facing in range(2):
                g = 2 * c + facing
                here = group16 == g
                turn = (16 * g - 16 * p) & 127
                turn_z = (16 * g - 16 * p + (-16 if facing else 16)) & 127
                parts = [
                    jnp.where(here, pltpu.roll(HX[facing, c], turn, 1), parts[0]),
                    jnp.where(here, pltpu.roll(HY[facing, c], turn, 1), parts[1]),
                    jnp.where(here, pltpu.roll(EF[facing, c], turn_z, 1), parts[2]),
                ]
        parts[2] = jnp.where(jnp.where(odd_group, p - 7, p) == 0, across, parts[2])
        rims.append(parts)
    for peer in range(peers):
        is_first = jnp.full(SLAB, groups[0], jnp.int32) == peer
        for k in range(3):
            MSG[peer, 16 * k : 16 * k + 16] = jnp.where(is_first, rims[0][k], rims[1][k])
        first = jnp.full(TILE, groups[0], jnp.int32) == peer
        second = jnp.full(TILE, groups[1], jnp.int32) == peer
        MSG[peer, 48:56] = jnp.where(first | second, 1.0, 0.0)
    out_rims = []
    for step in range(1, peers):
        peer = lax.rem(me + step, peers)
        out_rims.append(
            push(
                MSG.at[peer], RIM.at[step], bsend.at[step - 1], brecv.at[step - 1], beside(0, step)
            )
        )
        out_rims[-1].start()
    RIM[0] = MSG[me]

    def total(s, colour, c, j, weights):
        other = U.at[s, 1 - colour, c]
        tile = other[j + 1]
        return (
            LD[s, colour, c, j]
            + weights[0] * tile
            + weights[1] * far(colour, other[j], other[j + 2])
            + weights[2] * y_down(tile)
            + weights[3] * y_up(tile)
            + weights[4] * pltpu.roll(tile, 1, 1)
            + weights[5] * pltpu.roll(tile, 127, 1)
        )

    def one_slot(turn):
        s = turn
        if turn > 0:
            push(
                MSG.at[0], RIM.at[turn], bsend.at[turn - 1], brecv.at[turn - 1], beside(0, 1)
            ).wait_recv()

        high_half = quarter >= 2
        x_rows = [RIM[s, pl.ds(h, 8, stride=2), :] for h in range(2)]
        z_rows = [RIM[s, pl.ds(32 + h, 8, stride=2), :] for h in range(2)]
        y_slab = RIM[s, 16:32]
        rim_x = []
        for c in range(4):
            for facing in range(2):
                index = 16 * (2 * c + facing) + (third >> 1)
                ghost = jnp.where(
                    high_half, lane_take(x_rows[1], index), lane_take(x_rows[0], index)
                )
                if c == 3:
                    rim_x.append(ghost)
                else:
                    for colour in range(2):
                        U[s, colour, c, facing * 17] = ghost
            index = 32 * c + jnp.where((lane16 >> 5) == 3, 16, 0) + ((lane16 & 31) >> 1)
            GY[c] = lane_take(y_slab, index)
        for colour in range(2):
            for facing in range(2):
                j = (EDGE - 1) * facing
                at_rim = even if colour == facing else jnp.logical_not(even)
                more = jnp.where(at_rim, 0.5 * rim_x[facing], 0.0)
                W[s, colour, j, 1] = W[s, colour, j, 1] + more
                W[s, colour, j, 6] = W[s, colour, j, 6] + more

        at_z = z_first | z_last
        at_y = y_first | y_last

        def surround(big):
            stores = []
            for small in range(8):
                j = 8 * big + small
                ghost_z, ghost_y = [], []
                for c in range(4):
                    index = 32 * c + j + jnp.where(z_last, 16, 0)
                    ghost_z.append(
                        jnp.where(
                            high_half, lane_take(z_rows[1], index), lane_take(z_rows[0], index)
                        )
                    )
                    ghost_y.append(jnp.broadcast_to(GY[c, j : j + 1, :], TILE))
                for colour in range(2):
                    half = 0.5 * PV[s, colour, j + 1]
                    half_z, half_y = 0.5 * ghost_z[3], 0.5 * ghost_y[3]
                    rim_z = jnp.where(at_z, half + half_z, 0.0)
                    rim_y = jnp.where(at_y, half + half_y, 0.0)
                    diagonal = (
                        W[s, colour, j, 6]
                        + jnp.where(at_z, half_z, 0.0)
                        + jnp.where(at_y, half_y, 0.0)
                    )
                    loaded = [
                        LD[s, colour, c, j] + rim_y * ghost_y[c] + rim_z * ghost_z[c]
                        for c in range(3)
                    ]
                    stores.append((colour, j, diagonal, 1.0 / diagonal, loaded))
            for colour, j, diagonal, inverse, loaded in stores:
                W[s, colour, j, 6] = diagonal
                W[s, colour, j, 7] = inverse
                for c in range(3):
                    LD[s, colour, c, j] = loaded[c]

        for big in range(2):
            surround(big)

        def sweep(number, carry):
            for colour in range(2):
                stores = []
                for j in range(EDGE):
                    weights = [W[s, colour, j, k] for k in range(8)]
                    for c in range(3):
                        summed = total(s, colour, c, j, weights)
                        new = summed * weights[7]
                        left = summed - weights[6] * new if colour == 1 else None
                        stores.append((c, j, new, left))
                for c, j, new, left in stores:
                    U[s, colour, c, j + 1] = new
                    if colour == 1:
                        RB[c, j] = left
            return carry

        lax.fori_loop(0, SWEEPS, sweep, 0)


        even_z = (third & 1) == 0
        even_y = (quarter & 1) == 0
        stores = []
        for j in range(EDGE):
            weights = [W[s, 0, j, k] for k in range(7)]
            for c in range(3):
                left = total(s, 0, c, j, weights) - weights[6] * U[s, 0, c, j + 1]
                stores.append((c, j, left + RB[c, j]))
        for c, j, left in stores:
            RB[c, j] = left

        stores = []
        for big in range(4):
            for k in range(6):
                tiles = []
                for small in range(4):
                    j = 4 * big + small
                    if k < 3:
                        tiles.append(RB[k, j])
                    else:
                        tiles.append(U[s, 0, k - 3, j + 1] + U[s, 1, k - 3, j + 1])
                halves = []
                for h in range(2):
                    one, two = tiles[2 * h], tiles[2 * h + 1]
                    halves.append(
                        jnp.where(
                            even_z, one + pltpu.roll(one, 127, 1), two + pltpu.roll(two, 1, 1)
                        )
                    )
                mean = 0.125 * jnp.where(
                    even_y,
                    halves[0] + pltpu.roll(halves[0], 96, 1),
                    halves[1] + pltpu.roll(halves[1], 32, 1),
                )
                stores.append((6 * big + k, mean))
        for number, mean in stores:
            MEAN[s, number] = mean
        for h in range(2):
            index = (2 * h + ((lane & 3) >> 1)) * 32 + (lane & 1)
            index = index + jnp.where(((lane >> 4) & 1) == 0, 30, 0)
            end = jnp.zeros(TILE, jnp.float32)
            for big in range(4):
                for c in range(3):
                    here = (quarter == c) & (((lane & 15) >> 2) == big)
                    end = jnp.where(here, lane_take(MEAN[s, 6 * big + 3 + c], index), end)
            ZM[s, pl.ds(h, 8, stride=2), :] = end

        for way in range(6):
            if way < 2 and turn == 1 + 2 * way:
                RX[way, me] = MEAN[s, 21:24] if way == 0 else MEAN[s, 3:6]
            else:
                out_means.append(to_side(way, turn))
                out_means[-1].start()
        if turn > 0:
            out_means.append(
                push(
                    MEAN.at[turn], RET.at[turn], csend.at[turn - 1], crecv.at[turn - 1],
                    beside(0, -turn),
                )
            )
            out_means[-1].start()

    def to_side(way, turn):
        sems = dsend.at[4 * way + turn], drecv.at[4 * way + turn]
        step = 1 - 2 * (way & 1)
        if way < 2:
            tiles = MEAN.at[turn, 21:24] if way == 0 else MEAN.at[turn, 3:6]
            return push(tiles, RX.at[way, me], *sems, beside(0, step - turn))
        device = beside(way // 2, step) | beside(0, -turn)
        if way < 4:
            return push(MEAN.at[turn, :, 7 if way == 2 else 0], RY.at[way - 2, me], *sems, device)
        return push(ZM.at[turn], RZ.at[way - 4, me], *sems, device)

    out_means = []
    for turn in (0, 2, 1, 3):
        one_slot(turn)
    RET[0] = MEAN[0]

    def spell_out(j, carry):
        for turn in range(SLOTS):
            taken = RIM[turn, 48:56]
            slot = lax.rem(me + (peers - turn), peers)
            for c in range(3):
                red, black = U[turn, 0, c, j + 1], U[turn, 1, c, j + 1]
                start = c * 1024 + 64 * j + slot
                rows = pl.ds(start, 8, stride=SLOTS)
                fo[rows, :] = jnp.where(even, red, black) * taken
                rows = pl.ds(start + 32, 8, stride=SLOTS)
                fo[rows, :] = jnp.where(even, black, red) * taken
        return carry

    lax.fori_loop(0, EDGE, spell_out, 0)
    for facing in range(2):
        for c in range(4):
            C[c, facing * 17] = HX[facing, c]
    loads[5].wait()
    for turn in range(1, peers):
        push(
            MEAN.at[turn], RET.at[turn], csend.at[turn - 1], crecv.at[turn - 1], beside(0, -turn)
        ).wait_recv()
    senders = [lax.rem(groups[i] + (peers - me), peers) for i in range(2)]
    for i in range(2):
        for number in range(24):
            RS[i, number] = RET[senders[i], number]
    for turn in range(peers):
        for way in range(6):
            if way < 2 and turn == 1 + 2 * way:
                continue
            step = 0 if way >= 2 else 2 * way - 1
            owner_at = lax.rem(me + (turn + step + peers), peers)
            sems = dsend.at[4 * way + turn], drecv.at[4 * way + turn]
            if way < 2:
                pair = MEAN.at[0, 0:3], RX.at[way, owner_at]
            elif way < 4:
                pair = MEAN.at[0, :, 0], RY.at[way - 2, owner_at]
            else:
                pair = ZM.at[0], RZ.at[way - 4, owner_at]
            push(*pair, *sems, beside(1, 1)).wait_recv()

    for copy in outward + out_rims + out_means:
        copy.wait_send()


def write_out(
    fine, C, CR, HX, HY, HZ, RX, RY, RZ, RS, M, fo, so, ro, SP, RM, HYN, HZN, R, sem
):
    copies = [
        pltpu.make_async_copy(SP.at[:, 1 : EDGE + 1], so, sem.at[0]),
        pltpu.make_async_copy(fine, fo, sem.at[1]),
        pltpu.make_async_copy(R, ro, sem.at[2]),
    ]
    copies[1].start()
    lane = lax.broadcasted_iota(jnp.int32, TILE, 1)
    refined = [M[i, 0:8] > 0.5 for i in range(2)]

    def sources(small, h, lanes):
        return (2 * h + (small >> 1)) * 32 + (small & 1) + 2 * (lanes & 15)

    for big in range(4):
        stores = []
        for k in range(6):
            first = RS[0, 6 * big + k]
            second = RS[1, 6 * big + k]
            for small in range(4):
                x = 4 * big + small
                for h in range(2):
                    index = sources(small, h, lane)
                    rows = pl.ds(h, 8, stride=2)
                    value = jnp.where(refined[0], lane_take(first, index), lane_take(second, index))
                    if k >= 3:
                        base = C[k - 3, x + 1, rows, :]
                        value = jnp.where(refined[0] | refined[1], value, base)
                    stores.append((k, x, rows, value))
        for k, x, rows, value in stores:
            if k >= 3:
                SP[k - 3, x + 1, rows, :] = value
            else:
                RM[k, x, rows, :] = value
    copies[0].start()

    def chosen(mark, base, values):
        for number, value in enumerate(values):
            base = jnp.where(mark == number + 1.0, value, base)
        return base

    stores = []
    for facing in range(2):
        mark = HX[facing, 4, 0:8]
        for h in range(2):
            rows = pl.ds(h, 8, stride=2)
            index = sources(3 - 3 * facing, h, lane)
            for c in range(3):
                values = [lane_take(RX[facing, number, c], index) for number in range(SLOTS)]
                stores.append((facing, c, rows, chosen(mark, HX[facing, c, rows, :], values)))
    for facing, c, rows, value in stores:
        SP[c, facing * 17, rows, :] = value
    tall = (24, 128)
    for facing in range(2):
        mark = jnp.broadcast_to(HY[facing, 4, 0:1], tall)
        for small in range(4):
            index = sources(small, 1 - facing, lax.broadcasted_iota(jnp.int32, tall, 1))
            values = [lane_take(RY[facing, number], index) for number in range(SLOTS)]
            HYN[facing, small] = chosen(mark, jnp.zeros(tall, jnp.float32), values)
        HZN[facing] = chosen(
            HZ[facing, 16:32], HZ[facing, 0:16], [RZ[facing, number] for number in range(SLOTS)]
        )
    near_refined = [HY[facing, 4] > 0.5 for facing in range(2)]

    lane16 = lax.broadcasted_iota(jnp.int32, SLAB, 1)
    row16 = lax.broadcasted_iota(jnp.int32, SLAB, 0)
    refined_here = (M[0] + M[1]) > 0.5

    def leftover(big):
        def neighbours(block, c, x, hz):
            centre = block[c, x + 1]
            lanes = [
                lane_take(hz[f, 0:16], jnp.full(SLAB, 32 * c + 16 * f, jnp.int32) + x) for f in range(2)
            ]
            rows = [jnp.broadcast_to(HY[f, c, pl.ds(x, 1), :], SLAB) for f in range(2)]
            if c < 3:
                row = 6 * (x >> 2) + 3 + c
                news = [HYN[f, x & 3, pl.ds(row, 1), :] for f in range(2)]
                rows = [
                    jnp.where(near_refined[f], jnp.broadcast_to(news[f], SLAB), rows[f])
                    for f in range(2)
                ]
            return centre, [
                block[c, x],
                block[c, x + 2],
                jnp.where(row16 == 0, rows[0], pltpu.roll(centre, 1, 0)),
                jnp.where(row16 == 15, rows[1], pltpu.roll(centre, 15, 0)),
                jnp.where(lane16 == 0, lanes[0], pltpu.roll(centre, 1, 1)),
                jnp.where(lane16 == 127, lanes[1], pltpu.roll(centre, 127, 1)),
            ]

        stores = []
        for small in range(8):
            x = 8 * big + small
            centre, near = neighbours(C, 3, x, HZ)
            face = [0.5 * (centre + value) for value in near]
            for c in range(3):
                centre, near = neighbours(SP, c, x, HZN)
                applied = face[0] * (centre - near[0])
                for k in range(1, 6):
                    applied = applied + face[k] * (centre - near[k])
                left = CR[c, x] - (REACTION * centre + 0.25 * applied)
                stores.append((c, x, jnp.where(refined_here, RM[c, x], left)))
        for c, x, left in stores:
            R[c, x] = left

    for big in range(EDGE // 8):
        leftover(big)
    copies[2].start()
    for copy in copies:
        copy.wait()


def shards(cv, cm, cr, fv, fr, fm, refined, owner):
    def rows_of(values):
        return values[0].transpose(1, 0, 2).reshape(3, SLOTS, 256, 128).transpose(
            0, 2, 1, 3
        ).reshape(3072, 128)

    f32 = jnp.float32
    vmem = lambda *shape: pltpu.VMEM(shape, f32)
    dma = lambda count: pltpu.SemaphoreType.DMA((count,))
    any_space = pl.BlockSpec(memory_space=pltpu.HBM)
    in_vmem = pl.BlockSpec(memory_space=pltpu.VMEM)
    shape = jax.ShapeDtypeStruct
    here = lambda x: pltpu.with_memory_space_constraint(x, pltpu.HBM)
    kept = [
        (3072, 128),
        (5, 18, 16, 128),
        (3, 16, 16, 128),
        (2, 5, 16, 128),
        (2, 5, 16, 128),
        (2, 32, 128),
        (2, 4, 3, 8, 128),
        (2, 4, 24, 128),
        (2, 4, 16, 128),
        (2, 24, 8, 128),
        (2, 16, 128),
    ]
    held = pl.pallas_call(
        kernel,
        name="smooth",
        out_shape=[vmem(*dims) for dims in kept],
        in_specs=[any_space] * 8,
        out_specs=[in_vmem] * len(kept),
        scratch_shapes=[
            vmem(3072, 128),
            vmem(3072, 128),
            vmem(1024, 128),
            vmem(2, 4, 16, 128),
            vmem(32, 128),
            vmem(4, 56, 128),
            vmem(4, 56, 128),
            vmem(4, 2, 18, 8, 128),
            vmem(4, 2, 3, 18, 8, 128),
            vmem(4, 2, 3, 16, 8, 128),
            vmem(4, 2, 16, 8, 8, 128),
            vmem(4, 16, 128),
            vmem(3, 16, 8, 128),
            vmem(4, 24, 8, 128),
            vmem(4, 24, 8, 128),
            vmem(4, 16, 128),
            pltpu.SMEM((1, 2), jnp.int32),
            pltpu.SMEM((1, 2), jnp.int32),
            dma(8), dma(6), dma(6), dma(3), dma(3), dma(3), dma(3), dma(24), dma(24),
        ],
        compiler_params=pltpu.CompilerParams(
            collective_id=0, has_side_effects=True, vmem_limit_bytes=48 * 2**20
        ),
    )(
        here(cv), here(cm), here(cr), here(rows_of(fv)), here(rows_of(fr)),
        here(fm[0].reshape(SLOTS, 256, 128).transpose(1, 0, 2).reshape(1024, 128)),
        here(refined), here(owner),
    )
    fine, synced, residual = pl.pallas_call(
        write_out,
        name="write_out",
        out_shape=[
            shape((3072, 128), f32),
            shape((3, 16, 16, 128), f32),
            shape((3, 16, 16, 128), f32),
        ],
        in_specs=[in_vmem] * len(kept),
        out_specs=[any_space] * 3,
        scratch_shapes=[
            vmem(3, 18, 16, 128),
            vmem(3, 16, 16, 128),
            vmem(2, 4, 24, 128),
            vmem(2, 16, 128),
            vmem(3, 16, 16, 128),
            dma(3),
        ],
    )(*(pltpu.with_memory_space_constraint(x, pltpu.VMEM) for x in held))
    fine = fine.reshape(3, 256, SLOTS, 128).transpose(0, 2, 1, 3).reshape(3, SLOTS, 32768)
    return fine.transpose(1, 0, 2)[None], synced, residual


def solution(mesh):
    block = P(None, "gx", "gy", "gz")
    slots = P(("gx", "gy", "gz"))
    return jax.shard_map(
        shards,
        mesh=mesh,
        in_specs=(block, P("gx", "gy", "gz"), block, slots, slots, slots, slots, slots),
        out_specs=(slots, block, block),
        check_vma=False,
    )
```

```python
import functools

import jax
import jax.numpy as jnp
from jax import lax
from jax.experimental import pallas as pl
from jax.experimental.pallas import tpu as pltpu
from jax.sharding import PartitionSpec as P

SWEEPS = 2
EDGE = 16
SLOTS = 4
REACTION = 1.0
TILE = (8, 128)
SLAB = (16, 128)
MESH = pl.DeviceIdType.MESH
AXES = ("gx", "gy", "gz")


def lane_take(values, index):
    numbers = lax.GatherDimensionNumbers(
        offset_dims=(),
        collapsed_slice_dims=(1,),
        start_index_map=(1,),
        operand_batching_dims=(0,),
        start_indices_batching_dims=(0,),
    )
    return lax.gather(
        values,
        index[..., None],
        numbers,
        slice_sizes=(1, 1),
        mode=lax.GatherScatterMode.PROMISE_IN_BOUNDS,
    )


def push(source, target, sent, landed, device):
    return pltpu.make_async_remote_copy(
        src_ref=source,
        dst_ref=target,
        send_sem=sent,
        recv_sem=landed,
        device_id=device,
        device_id_type=MESH,
    )


def kernel(
    cv, cm, cr, fv, fr, fm, place_in, own_in,
    fo, C, CR, HX, HY, HZ, RX, RY, RZ, RSV, RSR, M,
    FV, FR, FM, EF, ZF, MSG, RIM, PV, U, LD, W, GY, RB,
    MV, MR, RETV, RETR, ZM, place, own,
    lsem, asend, arecv, bsend, brecv, csend, crecv, dsend, drecv,
):
    at = [lax.axis_index(axis) for axis in AXES]
    size = [lax.axis_size(axis) for axis in AXES]
    me, peers = at[0], size[0]

    def beside(number, step):
        return {AXES[number]: lax.rem(at[number] + (step + size[number]), size[number])}

    loads = [
        pltpu.make_async_copy(cv, C.at[0:3, 1 : EDGE + 1], lsem.at[0]),
        pltpu.make_async_copy(cm, C.at[3, 1 : EDGE + 1], lsem.at[1]),
        pltpu.make_async_copy(fm, FM, lsem.at[2]),
        pltpu.make_async_copy(fr, FR, lsem.at[3]),
        pltpu.make_async_copy(fv, FV, lsem.at[4]),
        pltpu.make_async_copy(cr, CR, lsem.at[5]),
        pltpu.make_async_copy(place_in, place, lsem.at[6]),
        pltpu.make_async_copy(own_in, own, lsem.at[7]),
    ]
    for number in (6, 7, 0, 1, 2, 3, 4, 5):
        loads[number].start()

    barrier = pltpu.get_barrier_semaphore()
    for number in range(3):
        for step in (1, -1):
            pl.semaphore_signal(
                barrier, inc=1, device_id=beside(number, step), device_id_type=MESH
            )
    lane = lax.broadcasted_iota(jnp.int32, TILE, 1)
    row = lax.broadcasted_iota(jnp.int32, TILE, 0)
    third = lane & 31
    quarter = lane >> 5
    even = ((third + quarter) & 1) == 0
    z_first, z_last = third == 0, third == 31
    y_first = (row == 0) & (quarter == 0)
    y_last = (row == 7) & (quarter == 3)
    lane16 = lax.broadcasted_iota(jnp.int32, SLAB, 1)
    row16 = lax.broadcasted_iota(jnp.int32, SLAB, 0)
    group16 = lane16 >> 4
    inner16 = lane16 & 15

    loads[6].wait()
    loads[7].wait()
    positions = [place[0, 0], place[0, 1]]
    groups = [lax.div(own[0, i], size[1] * size[2]) for i in range(2)]
    marks = [(groups[i] + 1).astype(jnp.float32) for i in range(2)]

    def marked(numbers, wanted):
        return jnp.where(
            numbers[0] == wanted, marks[0], jnp.where(numbers[1] == wanted, marks[1], 0.0)
        )

    spots = [jnp.full(SLAB, positions[i], jnp.int32) for i in range(2)]
    mark = marked(spots, group16)
    for x in range(EDGE):
        C[4, x + 1] = mark
    ZF[16:32] = jnp.where((group16 & 1) == 1, marked(spots, 0), marked(spots, 7))
    for i in range(2):
        M[i] = jnp.where(group16 == positions[i], 1.0, 0.0)

    loads[0].wait()
    loads[1].wait()
    packed = jnp.zeros(SLAB, jnp.float32)
    for c in range(4):
        upper = jnp.zeros(SLAB, jnp.float32)
        lower = jnp.zeros(SLAB, jnp.float32)
        for x in range(EDGE):
            plane = C[c, x + 1]
            here = inner16 == x
            upper = jnp.where(here, pltpu.roll(plane, (x - 15) % 128, 1), upper)
            lower = jnp.where(here, pltpu.roll(plane, x, 1), lower)
        EF[0, c] = upper
        EF[1, c] = lower
        turn = (32 * c + 16) % 128
        packed = jnp.where(group16 == 2 * c, pltpu.roll(upper, turn, 1), packed)
        packed = jnp.where(group16 == 2 * c + 1, pltpu.roll(lower, turn, 1), packed)
    ZF[0:16] = packed
    pl.semaphore_wait(barrier, 6)
    inner = pl.ds(1, EDGE)
    outward = [
        push(C.at[:, EDGE], HX.at[0], asend.at[0], arecv.at[0], beside(0, 1)),
        push(C.at[:, 1], HX.at[1], asend.at[1], arecv.at[1], beside(0, -1)),
        push(C.at[:, inner, EDGE - 1], HY.at[0], asend.at[2], arecv.at[2], beside(1, 1)),
        push(C.at[:, inner, 0], HY.at[1], asend.at[3], arecv.at[3], beside(1, -1)),
        push(ZF, HZ.at[0], asend.at[4], arecv.at[4], beside(2, 1)),
        push(ZF, HZ.at[1], asend.at[5], arecv.at[5], beside(2, -1)),
    ]
    for copy in outward:
        copy.start()

    loads[2].wait()
    loads[3].wait()
    loads[4].wait()

    def pack(j, carry):
        def pair(ref, start):
            low = ref[pl.ds(start + 64 * j, 8, stride=SLOTS), :]
            high = ref[pl.ds(start + 64 * j + 32, 8, stride=SLOTS), :]
            return jnp.where(even, low, high), jnp.where(even, high, low)

        for s in range(SLOTS):
            slot = lax.rem(me + (peers - s), peers)
            PV[s, 0, j + 1], PV[s, 1, j + 1] = pair(FM, slot)
            for c in range(3):
                LD[s, 0, c, j], LD[s, 1, c, j] = pair(FR, c * 1024 + slot)
                rows = pl.ds(pl.multiple_of(8 * j + 8, 8), 8)
                U[s, 0, c, rows], U[s, 1, c, rows] = pair(FV, c * 1024 + slot)
        return carry

    def y_up(tile):
        turned = pltpu.roll(tile, 96, 1)
        return jnp.where(quarter == 3, pltpu.roll(turned, 7, 0), turned)

    def y_down(tile):
        turned = pltpu.roll(tile, 32, 1)
        return jnp.where(quarter == 0, pltpu.roll(turned, 1, 0), turned)

    def far(colour, before, after):
        if colour == 0:
            return jnp.where(even, before, after)
        return jnp.where(even, after, before)

    def prepare(step, carry):
        s, big = step >> 2, step & 3
        stores = []
        for small in range(4):
            j = 4 * big + small
            for colour in range(2):
                own_tile = PV[s, colour, j + 1]
                other = PV.at[s, 1 - colour]
                tile = other[j + 1]
                face = [
                    0.5 * (own_tile + value)
                    for value in (
                        tile,
                        far(colour, other[j], other[j + 2]),
                        jnp.where(y_first, 0.0, y_down(tile)),
                        jnp.where(y_last, 0.0, y_up(tile)),
                        jnp.where(z_first, 0.0, pltpu.roll(tile, 1, 1)),
                        jnp.where(z_last, 0.0, pltpu.roll(tile, 127, 1)),
                    )
                ]
                diagonal = REACTION + face[0]
                for value in face[1:]:
                    diagonal = diagonal + value
                inside = face[:2] + [
                    jnp.where(outer, 0.0, value)
                    for outer, value in zip((y_first, y_last, z_first, z_last), face[2:])
                ]
                stores.append((colour, j, inside + [diagonal]))
        for colour, j, values in stores:
            for k, value in enumerate(values):
                W[s, colour, j, k] = value
        return carry

    for s in range(SLOTS):
        for colour in range(2):
            for end in (0, EDGE + 1):
                PV[s, colour, end] = jnp.zeros(TILE, jnp.float32)
    lax.fori_loop(0, EDGE, pack, 0)
    lax.fori_loop(0, EDGE, prepare, 0)

    for copy in outward:
        copy.wait_recv()
    for number, halo in ((0, HX), (1, HY)):
        for facing in range(2):
            outside = at[number] == (size[number] - 1 if facing else 0)
            halo[facing] = jnp.where(outside, 0.0, halo[facing])
    for facing in range(2):
        outside = at[2] == (size[2] - 1 if facing else 0)
        HZ[facing] = jnp.where(outside, 0.0, HZ[facing])

    odd_group = (group16 & 1) == 1
    across = jnp.where(odd_group, HZ[1, 0:16], HZ[0, 0:16])
    rims = []
    for i in range(2):
        p = positions[i]
        parts = [jnp.zeros(SLAB, jnp.float32)] * 3
        for c in range(4):
            for facing in range(2):
                g = 2 * c + facing
                here = group16 == g
                turn = (16 * g - 16 * p) & 127
                turn_z = (16 * g - 16 * p + (-16 if facing else 16)) & 127
                parts = [
                    jnp.where(here, pltpu.roll(HX[facing, c], turn, 1), parts[0]),
                    jnp.where(here, pltpu.roll(HY[facing, c], turn, 1), parts[1]),
                    jnp.where(here, pltpu.roll(EF[facing, c], turn_z, 1), parts[2]),
                ]
        parts[2] = jnp.where(jnp.where(odd_group, p - 7, p) == 0, across, parts[2])
        rims.append(parts)
    for peer in range(peers):
        is_first = jnp.full(SLAB, groups[0], jnp.int32) == peer
        for k in range(3):
            MSG[peer, 16 * k : 16 * k + 16] = jnp.where(is_first, rims[0][k], rims[1][k])
        first = jnp.full(TILE, groups[0], jnp.int32) == peer
        second = jnp.full(TILE, groups[1], jnp.int32) == peer
        MSG[peer, 48:56] = jnp.where(first | second, 1.0, 0.0)
    out_rims = []
    for step in range(1, peers):
        peer = lax.rem(me + step, peers)
        out_rims.append(
            push(
                MSG.at[peer], RIM.at[step], bsend.at[step - 1], brecv.at[step - 1], beside(0, step)
            )
        )
        out_rims[-1].start()
    RIM[0] = MSG[me]

    def total(s, colour, c, j, weights):
        other = U.at[s, 1 - colour, c]
        at_row = 8 * j + 8
        tile = other[at_row : at_row + 8]
        behind, ahead = other[at_row - 1 : at_row + 7], other[at_row + 1 : at_row + 9]
        return (
            LD[s, colour, c, j]
            + weights[0] * tile
            + weights[1] * far(colour, other[at_row - 8 : at_row], other[at_row + 8 : at_row + 16])
            + weights[2] * pltpu.roll(jnp.where(quarter == 3, behind, tile), 32, 1)
            + weights[3] * pltpu.roll(jnp.where(quarter == 0, ahead, tile), 96, 1)
            + weights[4] * pltpu.roll(tile, 1, 1)
            + weights[5] * pltpu.roll(tile, 127, 1)
        )

    def one_slot(turn):
        s = turn
        if turn > 0:
            push(
                MSG.at[0], RIM.at[turn], bsend.at[turn - 1], brecv.at[turn - 1], beside(0, 1)
            ).wait_recv()

        high_half = quarter >= 2
        x_rows = [RIM[s, pl.ds(h, 8, stride=2), :] for h in range(2)]
        z_rows = [RIM[s, pl.ds(32 + h, 8, stride=2), :] for h in range(2)]
        y_slab = RIM[s, 16:32]
        rim_x = []
        for c in range(4):
            for facing in range(2):
                index = 16 * (2 * c + facing) + (third >> 1)
                ghost = jnp.where(
                    high_half, lane_take(x_rows[1], index), lane_take(x_rows[0], index)
                )
                if c == 3:
                    rim_x.append(ghost)
                else:
                    for colour in range(2):
                        U[s, colour, c, facing * 136 : facing * 136 + 8] = ghost
            index = 32 * c + jnp.where((lane16 >> 5) == 3, 16, 0) + ((lane16 & 31) >> 1)
            GY[c] = lane_take(y_slab, index)
        for colour in range(2):
            for facing in range(2):
                j = (EDGE - 1) * facing
                at_rim = even if colour == facing else jnp.logical_not(even)
                more = jnp.where(at_rim, 0.5 * rim_x[facing], 0.0)
                W[s, colour, j, 1] = W[s, colour, j, 1] + more
                W[s, colour, j, 6] = W[s, colour, j, 6] + more

        at_z = z_first | z_last
        at_y = y_first | y_last

        def surround(big):
            stores = []
            for small in range(8):
                j = 8 * big + small
                ghost_z, ghost_y = [], []
                for c in range(4):
                    index = 32 * c + j + jnp.where(z_last, 16, 0)
                    ghost_z.append(
                        jnp.where(
                            high_half, lane_take(z_rows[1], index), lane_take(z_rows[0], index)
                        )
                    )
                    ghost_y.append(jnp.broadcast_to(GY[c, j : j + 1, :], TILE))
                for colour in range(2):
                    half = 0.5 * PV[s, colour, j + 1]
                    half_z, half_y = 0.5 * ghost_z[3], 0.5 * ghost_y[3]
                    rim_z = jnp.where(at_z, half + half_z, 0.0)
                    rim_y = jnp.where(at_y, half + half_y, 0.0)
                    diagonal = (
                        W[s, colour, j, 6]
                        + jnp.where(at_z, half_z, 0.0)
                        + jnp.where(at_y, half_y, 0.0)
                    )
                    loaded = [
                        LD[s, colour, c, j] + rim_y * ghost_y[c] + rim_z * ghost_z[c]
                        for c in range(3)
                    ]
                    stores.append((colour, j, diagonal, 1.0 / diagonal, loaded))
            for colour, j, diagonal, inverse, loaded in stores:
                W[s, colour, j, 6] = diagonal
                W[s, colour, j, 7] = inverse
                for c in range(3):
                    LD[s, colour, c, j] = loaded[c]

        for big in range(2):
            surround(big)

        def sweep(number, carry):
            for colour in range(2):
                stores = []
                for j in range(EDGE):
                    weights = [W[s, colour, j, k] for k in range(8)]
                    for c in range(3):
                        summed = total(s, colour, c, j, weights)
                        new = summed * weights[7]
                        left = summed - weights[6] * new if colour == 1 else None
                        stores.append((c, j, new, left))
                for c, j, new, left in stores:
                    U[s, colour, c, 8 * j + 8 : 8 * j + 16] = new
                    if colour == 1:
                        RB[c, j] = left
            return carry

        lax.fori_loop(0, SWEEPS, sweep, 0)


        even_z = (third & 1) == 0
        even_y = (quarter & 1) == 0
        def mean_of(tiles):
            halves = []
            for h in range(2):
                one, two = tiles[2 * h], tiles[2 * h + 1]
                halves.append(
                    jnp.where(even_z, one + pltpu.roll(one, 127, 1), two + pltpu.roll(two, 1, 1))
                )
            return 0.125 * jnp.where(
                even_y,
                halves[0] + pltpu.roll(halves[0], 96, 1),
                halves[1] + pltpu.roll(halves[1], 32, 1),
            )

        def to_home(tiles, back, number):
            sems = csend.at[number], crecv.at[number]
            out_means.append(push(tiles.at[turn], back.at[turn], *sems, beside(0, -turn)))
            out_means[-1].start()

        means = []
        for big in range(4):
            for c in range(3):
                tiles = []
                for j in range(4 * big, 4 * big + 4):
                    rows = slice(8 * j + 8, 8 * j + 16)
                    tiles.append(U[s, 0, c, rows] + U[s, 1, c, rows])
                means.append(mean_of(tiles))
        for number, mean in enumerate(means):
            MV[s, number] = mean
        for h in range(2):
            index = (2 * h + ((lane & 3) >> 1)) * 32 + (lane & 1)
            index = index + jnp.where(((lane >> 4) & 1) == 0, 30, 0)
            end = jnp.zeros(TILE, jnp.float32)
            for big in range(4):
                for c in range(3):
                    here = (quarter == c) & (((lane & 15) >> 2) == big)
                    end = jnp.where(here, lane_take(means[3 * big + c], index), end)
            ZM[s, pl.ds(h, 8, stride=2), :] = end

        for way in range(6):
            if way < 2 and turn == 1 + 2 * way:
                RX[way, me] = MV[s, 9:12] if way == 0 else MV[s, 0:3]
            else:
                out_means.append(to_side(way, turn))
                out_means[-1].start()
        if turn > 0:
            to_home(MV, RETV, turn - 1)

        stores = []
        for j in range(EDGE):
            weights = [W[s, 0, j, k] for k in range(7)]
            for c in range(3):
                red = U[s, 0, c, 8 * j + 8 : 8 * j + 16]
                left = total(s, 0, c, j, weights) - weights[6] * red
                stores.append((c, j, left + RB[c, j]))
        for c, j, left in stores:
            RB[c, j] = left
        means = []
        for big in range(4):
            for c in range(3):
                means.append(mean_of([RB[c, 4 * big + i] for i in range(4)]))
        for number, mean in enumerate(means):
            MR[s, number] = mean
        if turn > 0:
            to_home(MR, RETR, turn + 2)

    def to_side(way, turn):
        sems = dsend.at[4 * way + turn], drecv.at[4 * way + turn]
        step = 1 - 2 * (way & 1)
        if way < 2:
            tiles = MV.at[turn, 9:12] if way == 0 else MV.at[turn, 0:3]
            return push(tiles, RX.at[way, me], *sems, beside(0, step - turn))
        device = beside(way // 2, step) | beside(0, -turn)
        if way < 4:
            return push(MV.at[turn, :, 7 if way == 2 else 0], RY.at[way - 2, me], *sems, device)
        return push(ZM.at[turn], RZ.at[way - 4, me], *sems, device)

    out_means = []
    for turn in (0, 3, 2, 1):
        one_slot(turn)
    RETV[0] = MV[0]
    RETR[0] = MR[0]

    def spell_out(j, carry):
        for turn in range(SLOTS):
            taken = RIM[turn, 48:56]
            slot = lax.rem(me + (peers - turn), peers)
            for c in range(3):
                rows = pl.ds(pl.multiple_of(8 * j + 8, 8), 8)
                red, black = U[turn, 0, c, rows], U[turn, 1, c, rows]
                start = c * 1024 + 64 * j + slot
                rows = pl.ds(start, 8, stride=SLOTS)
                fo[rows, :] = jnp.where(even, red, black) * taken
                rows = pl.ds(start + 32, 8, stride=SLOTS)
                fo[rows, :] = jnp.where(even, black, red) * taken
        return carry

    lax.fori_loop(0, EDGE, spell_out, 0)
    for facing in range(2):
        for c in range(4):
            C[c, facing * 17] = HX[facing, c]
    loads[5].wait()
    for turn in range(1, peers):
        for tiles, back, number in ((MV, RETV, turn - 1), (MR, RETR, turn + 2)):
            sems = csend.at[number], crecv.at[number]
            push(tiles.at[turn], back.at[turn], *sems, beside(0, -turn)).wait_recv()
    senders = [lax.rem(groups[i] + (peers - me), peers) for i in range(2)]
    for i in range(2):
        for number in range(12):
            RSV[i, number] = RETV[senders[i], number]
            RSR[i, number] = RETR[senders[i], number]
    for turn in range(peers):
        for way in range(6):
            if way < 2 and turn == 1 + 2 * way:
                continue
            step = 0 if way >= 2 else 2 * way - 1
            owner_at = lax.rem(me + (turn + step + peers), peers)
            sems = dsend.at[4 * way + turn], drecv.at[4 * way + turn]
            if way < 2:
                pair = MV.at[0, 0:3], RX.at[way, owner_at]
            elif way < 4:
                pair = MV.at[0, :, 0], RY.at[way - 2, owner_at]
            else:
                pair = ZM.at[0], RZ.at[way - 4, owner_at]
            push(*pair, *sems, beside(1, 1)).wait_recv()

    for copy in outward + out_rims + out_means:
        copy.wait_send()


def write_out(
    fine, C, CR, HX, HY, HZ, RX, RY, RZ, RSV, RSR, M, fo, so, ro, SP, RM, HYN, HZN, R, sem
):
    copies = [
        pltpu.make_async_copy(SP.at[:, 1 : EDGE + 1], so, sem.at[0]),
        pltpu.make_async_copy(fine, fo, sem.at[1]),
        pltpu.make_async_copy(R, ro, sem.at[2]),
    ]
    copies[1].start()
    lane = lax.broadcasted_iota(jnp.int32, TILE, 1)
    refined = [M[i, 0:8] > 0.5 for i in range(2)]

    def sources(small, h, lanes):
        return (2 * h + (small >> 1)) * 32 + (small & 1) + 2 * (lanes & 15)

    for big in range(4):
        stores = []
        for k in range(6):
            held, number = (RSV, 3 * big + k - 3) if k >= 3 else (RSR, 3 * big + k)
            first, second = held[0, number], held[1, number]
            for small in range(4):
                x = 4 * big + small
                for h in range(2):
                    index = sources(small, h, lane)
                    rows = pl.ds(h, 8, stride=2)
                    value = jnp.where(refined[0], lane_take(first, index), lane_take(second, index))
                    if k >= 3:
                        base = C[k - 3, x + 1, rows, :]
                        value = jnp.where(refined[0] | refined[1], value, base)
                    stores.append((k, x, rows, value))
        for k, x, rows, value in stores:
            if k >= 3:
                SP[k - 3, x + 1, rows, :] = value
            else:
                RM[k, x, rows, :] = value
    copies[0].start()

    def chosen(mark, base, values):
        for number, value in enumerate(values):
            base = jnp.where(mark == number + 1.0, value, base)
        return base

    stores = []
    for facing in range(2):
        mark = HX[facing, 4, 0:8]
        for h in range(2):
            rows = pl.ds(h, 8, stride=2)
            index = sources(3 - 3 * facing, h, lane)
            for c in range(3):
                values = [lane_take(RX[facing, number, c], index) for number in range(SLOTS)]
                stores.append((facing, c, rows, chosen(mark, HX[facing, c, rows, :], values)))
    for facing, c, rows, value in stores:
        SP[c, facing * 17, rows, :] = value
    for facing in range(2):
        mark = HY[facing, 4, 0:8]
        for small in range(4):
            index = sources(small, 1 - facing, lane)
            for part in (slice(0, 8), slice(4, 12)):
                values = [lane_take(RY[facing, number, part], index) for number in range(SLOTS)]
                HYN[facing, small, part] = chosen(mark, jnp.zeros(TILE, jnp.float32), values)
        HZN[facing] = chosen(
            HZ[facing, 16:32], HZ[facing, 0:16], [RZ[facing, number] for number in range(SLOTS)]
        )
    near_refined = [HY[facing, 4] > 0.5 for facing in range(2)]

    lane16 = lax.broadcasted_iota(jnp.int32, SLAB, 1)
    row16 = lax.broadcasted_iota(jnp.int32, SLAB, 0)
    refined_here = (M[0] + M[1]) > 0.5

    def leftover(big):
        def neighbours(block, c, x, hz):
            centre = block[c, x + 1]
            lanes = [
                lane_take(hz[f, 0:16], jnp.full(SLAB, 32 * c + 16 * f, jnp.int32) + x) for f in range(2)
            ]
            rows = [jnp.broadcast_to(HY[f, c, pl.ds(x, 1), :], SLAB) for f in range(2)]
            if c < 3:
                row = 3 * (x >> 2) + c
                news = [HYN[f, x & 3, row : row + 1, :] for f in range(2)]
                rows = [
                    jnp.where(near_refined[f], jnp.broadcast_to(news[f], SLAB), rows[f])
                    for f in range(2)
                ]
            return centre, [
                block[c, x],
                block[c, x + 2],
                jnp.where(row16 == 0, rows[0], pltpu.roll(centre, 1, 0)),
                jnp.where(row16 == 15, rows[1], pltpu.roll(centre, 15, 0)),
                jnp.where(lane16 == 0, lanes[0], pltpu.roll(centre, 1, 1)),
                jnp.where(lane16 == 127, lanes[1], pltpu.roll(centre, 127, 1)),
            ]

        stores = []
        for small in range(8):
            x = 8 * big + small
            centre, near = neighbours(C, 3, x, HZ)
            face = [0.5 * (centre + value) for value in near]
            for c in range(3):
                centre, near = neighbours(SP, c, x, HZN)
                applied = face[0] * (centre - near[0])
                for k in range(1, 6):
                    applied = applied + face[k] * (centre - near[k])
                left = CR[c, x] - (REACTION * centre + 0.25 * applied)
                stores.append((c, x, jnp.where(refined_here, RM[c, x], left)))
        for c, x, left in stores:
            R[c, x] = left

    for big in range(EDGE // 8):
        leftover(big)
    copies[2].start()
    for copy in copies:
        copy.wait()


def shards(cv, cm, cr, fv, fr, fm, refined, owner):
    def rows_of(values):
        return values[0].transpose(1, 0, 2).reshape(3, SLOTS, 256, 128).transpose(
            0, 2, 1, 3
        ).reshape(3072, 128)

    f32 = jnp.float32
    vmem = lambda *shape: pltpu.VMEM(shape, f32)
    dma = lambda count: pltpu.SemaphoreType.DMA((count,))
    any_space = pl.BlockSpec(memory_space=pltpu.HBM)
    in_vmem = pl.BlockSpec(memory_space=pltpu.VMEM)
    shape = jax.ShapeDtypeStruct
    here = lambda x: pltpu.with_memory_space_constraint(x, pltpu.HBM)
    kept = [
        (3072, 128),
        (5, 18, 16, 128),
        (3, 16, 16, 128),
        (2, 5, 16, 128),
        (2, 5, 16, 128),
        (2, 32, 128),
        (2, 4, 3, 8, 128),
        (2, 4, 12, 128),
        (2, 4, 16, 128),
        (2, 12, 8, 128),
        (2, 12, 8, 128),
        (2, 16, 128),
    ]
    held = pl.pallas_call(
        kernel,
        name="smooth",
        out_shape=[vmem(*dims) for dims in kept],
        in_specs=[any_space] * 8,
        out_specs=[in_vmem] * len(kept),
        scratch_shapes=[
            vmem(3072, 128),
            vmem(3072, 128),
            vmem(1024, 128),
            vmem(2, 4, 16, 128),
            vmem(32, 128),
            vmem(4, 56, 128),
            vmem(4, 56, 128),
            vmem(4, 2, 18, 8, 128),
            vmem(4, 2, 3, 144, 128),
            vmem(4, 2, 3, 16, 8, 128),
            vmem(4, 2, 16, 8, 8, 128),
            vmem(4, 16, 128),
            vmem(3, 16, 8, 128),
            vmem(4, 12, 8, 128),
            vmem(4, 12, 8, 128),
            vmem(4, 12, 8, 128),
            vmem(4, 12, 8, 128),
            vmem(4, 16, 128),
            pltpu.SMEM((1, 2), jnp.int32),
            pltpu.SMEM((1, 2), jnp.int32),
            dma(8), dma(6), dma(6), dma(3), dma(3), dma(6), dma(6), dma(24), dma(24),
        ],
        compiler_params=pltpu.CompilerParams(
            collective_id=0, has_side_effects=True, vmem_limit_bytes=48 * 2**20
        ),
    )(
        here(cv), here(cm), here(cr), here(rows_of(fv)), here(rows_of(fr)),
        here(fm[0].reshape(SLOTS, 256, 128).transpose(1, 0, 2).reshape(1024, 128)),
        here(refined), here(owner),
    )
    fine, synced, residual = pl.pallas_call(
        write_out,
        name="write_out",
        out_shape=[
            shape((3072, 128), f32),
            shape((3, 16, 16, 128), f32),
            shape((3, 16, 16, 128), f32),
        ],
        in_specs=[in_vmem] * len(kept),
        out_specs=[any_space] * 3,
        scratch_shapes=[
            vmem(3, 18, 16, 128),
            vmem(3, 16, 16, 128),
            vmem(2, 4, 16, 128),
            vmem(2, 16, 128),
            vmem(3, 16, 16, 128),
            dma(3),
        ],
    )(*(pltpu.with_memory_space_constraint(x, pltpu.VMEM) for x in held))
    fine = fine.reshape(3, 256, SLOTS, 128).transpose(0, 2, 1, 3).reshape(3, SLOTS, 32768)
    return fine.transpose(1, 0, 2)[None], synced, residual


def solution(mesh):
    block = P(None, "gx", "gy", "gz")
    slots = P(("gx", "gy", "gz"))
    return jax.shard_map(
        shards,
        mesh=mesh,
        in_specs=(block, P("gx", "gy", "gz"), block, slots, slots, slots, slots, slots),
        out_specs=(slots, block, block),
        check_vma=False,
    )
```
